256 devices in a mesh: row: 16 (over z_hi, y), col: 16 (over x, z_lo, core).
Axes of the slice: x: 4, y: 4, z: 8 (z_hi: 4, z_lo: 2; z = z_hi * 2 + z_lo), core: 2. Of those that a mesh axis runs over, the one named last changes fastest.
Arguments:
- opening_old: float32 [2048, 2048], P('row', 'col'), may hold values from 0.5 to 1.5
- pressure_old: float32 [2048, 2048], P('row', 'col'), may hold values from -4 to 4
- injection: float32 [2048, 2048], P('row', 'col'), may hold values from 0 to 2
- front_flags: int32 [16, 1024], P('row', 'col'), may hold values 0 or 1
- self_kernel: float32 [256, 256], replicated, may hold values from -0.375 to 0.375
- source_column: int32 [16, 1024, 4], P('row', 'col'), may hold values from 0 to 15, all different within a row; in each aligned block of 64 rows (0 to 63, 64 to 127, ..., all dimensions but the last counted through in order) at most 32 rows name the same one
- source_tile: int32 [16, 1024, 4], P('row', 'col'), may hold values from 0 to 63
- source_rank: int32 [16, 1024, 4], P('row', 'col'), may hold values from 1 to 16
- left_factor: float32 [16, 1024, 4, 16, 256], P('row', 'col'), may hold values from -1.5 to 1.5
- right_factor: float32 [16, 1024, 4, 16, 256], P('row', 'col'), may hold values from -0.375 to 0.375
Outputs:
- opening_new: float32 [2048, 2048], P('row', 'col')
- pressure_new: float32 [2048, 2048], P('row', 'col')
The draws below stay inside these ranges and needn't reach their ends.
Inputs may be any that keep to these rules, and one draw needn't show every extreme that they name: `source_column`: the 4 sources of a target tile lie in 4 different column blocks; among the 64 target tiles of one device no column block is named more than 32 times, and that count is reached.
All inputs are finite; a program needn't handle non-finite values. No bound on the sum of `front_flags` on one device may be relied on, other than what follows from the above.
Results may differ from the reference program's by a relative error of at most 0.000076.
Values sent between devices are 32-bit elements; how exact they have to be, the bound alone decides.
A program may use at most 64 MiB of HBM per device.

```python
import math
import jax
import jax.numpy as jnp
import numpy as np
from jax import lax

BR = 128
BC = 128
TSIDE = 16
NB = 4
RMAX = 16
PASSES = 3
TS = 256
T_DEV = 64
CAP = 32
NR = 2048
NC = 2048
BANDS = 16
TILE_COLS = 1024
N_ROW = 16
N_COL = 16


def set_ends(entries, stream_key, low, largest):
    extent = entries.shape
    index_at = [jax.random.randint(jax.random.fold_in(stream_key, axis), (), 0, extent[axis]) for axis in range(len(extent))]
    entries = entries.at[tuple(index_at)].set(low)
    longest = extent.index(max(extent))
    index_at[longest] = (index_at[longest] + 1) % extent[longest]
    return entries.at[tuple(index_at)].set(largest)


def block_levels(key, extent, shards, smallest, largest):
    loudness, own = 1.0, jax.random.fold_in(key, 6)
    for axis_at, shards_of in shards:
        draws = jnp.exp(jax.random.uniform(jax.random.fold_in(own, axis_at), (shards_of,), jnp.float32, smallest / len(shards), largest / len(shards)))
        loudness = loudness * jnp.repeat(draws, extent[axis_at] // shards_of).reshape([-1 if axis == axis_at else 1 for axis in range(len(extent))])
    return loudness


def deal_out(rng, own, number, rows, number_of, top, limit, slope):
    sequence = jax.random.permutation(rng, number_of)
    packed, ordinary = shares(number_of, rows * top, limit, slope, True), shares(number_of, rows * top, limit, slope, False)
    places = jnp.arange(number_of)

    def named(tallies, turn):
        used = int((tallies > 0).sum())
        fixed = max(1, used // 4)
        shifted = fixed + (places - fixed + turn * (used - fixed)) % max(1, number_of - fixed)
        return jnp.zeros((number_of,), jnp.int32).at[sequence[jnp.where(places < fixed, places, shifted)]].set(jnp.asarray(tallies, jnp.int32))

    tallies = jnp.where(number % 4 == 0, named(packed, number // 4), named(ordinary, number - number // 4 - 1))
    mixed = jax.random.permutation(jax.random.fold_in(own, 3), number_of)
    giver, sink = mixed[0:number_of // 2 * 2:2], mixed[1:number_of // 2 * 2:2]
    room = jnp.minimum(tallies[giver] - 1, limit - tallies[sink]) // 2
    room = jnp.where((giver == sequence[0]) | (sink == sequence[0]) | (tallies[sink] == 0), 0, jnp.maximum(room, 0))
    shifted = jax.random.randint(jax.random.fold_in(own, 4), (number_of // 2,), 0, 1 << 20) % (room + 1)
    tallies = tallies.at[giver].add(-shifted).at[sink].add(shifted)
    labels = jnp.searchsorted(jnp.cumsum(tallies), jnp.arange(rows * top), side="right").astype(jnp.int32)
    table = labels.reshape(top, rows).T
    table = table[jax.random.permutation(jax.random.fold_in(own, 1), rows)]
    turn = jax.random.randint(jax.random.fold_in(own, 2), (rows, 1), 0, top)
    return jnp.take_along_axis(table, (jnp.arange(top)[None, :] + turn) % top, axis=1)


def shares(count, total, limit, skew, full):
    portions = [(1 << 20) // math.isqrt(grade ** skew) + 1 for grade in range(1, count + 1)]
    largest = limit if full else min(limit, max(-(-total // count), total * portions[0] // sum(portions)))
    least = 1 if total - largest >= count - 1 else 0
    counts, surplus = [largest] + [least] * (count - 1), total - largest - least * (count - 1)
    while surplus > 0:
        free = [i for i in range(1, count) if counts[i] < largest] or [i for i in range(1, count) if counts[i] < limit]
        mass, left = sum([portions[i] for i in free]), surplus
        for i in free:
            extra = min(limit - counts[i], max(1, left * portions[i] // mass), surplus)
            counts[i] = counts[i] + extra
            surplus = surplus - extra
    return np.array(counts)


def bell_draw(own_key, dims, spread, reach, split=(), held_as=jnp.bfloat16):
    factor_of = block_levels(own_key, dims, split, -0.22, 0.18) if split else 1.0
    drawn = jax.random.normal(own_key, dims, jnp.float32) * spread * factor_of
    return jnp.minimum(jnp.maximum(drawn, -reach), reach).astype(held_as)


def setup_inputs(seed: int = 0) -> dict:
    keys = jax.random.split(jax.random.key(seed), 11)
    opening_old = jnp.clip(0.5 + 1.0 * jax.random.uniform(keys[0], (NR, NC), jnp.float32) ** block_levels(keys[0], (NR, NC), ((0, 16), (1, 16)), -0.2, 0.2), 0.5, 1.5)
    pressure_old = bell_draw(keys[1], (NR, NC), 1.0, 4.0, ((0, 16), (1, 16)), jnp.float32)
    injection = jnp.clip(2.0 * jax.random.uniform(keys[2], (NR, NC), jnp.float32) ** block_levels(keys[2], (NR, NC), ((0, 16), (1, 16)), -0.2, 0.2), 0.0, 2.0)
    front_flags = set_ends((jax.random.randint(keys[3], (BANDS, TILE_COLS), 0, 4) < 3).astype(jnp.int32), jax.random.fold_in(keys[3], 1), 0, 1)
    self_kernel = bell_draw(keys[4], (TS, TS), TS ** -0.5, 0.375, (), jnp.float32)
    source_column_keys = jax.random.split(jax.random.fold_in(keys[5], 1), BANDS * TILE_COLS // T_DEV)
    source_column_turns = jax.random.permutation(jax.random.fold_in(keys[5], 3), BANDS * TILE_COLS // T_DEV)
    source_column = jax.vmap(lambda own, number: deal_out(jax.random.fold_in(keys[5], 2), own, number, T_DEV, N_COL, NB, CAP, 2))(source_column_keys, source_column_turns).reshape((BANDS, TILE_COLS, NB))
    source_tile = set_ends(jax.random.randint(keys[6], (BANDS, TILE_COLS, NB), 0, T_DEV), jax.random.fold_in(keys[6], 1), 0, T_DEV - 1).astype(jnp.int32)
    source_rank = set_ends(jax.random.randint(keys[7], (BANDS, TILE_COLS, NB), 1, RMAX + 1), jax.random.fold_in(keys[7], 1), 1, RMAX).astype(jnp.int32)
    left_factor = bell_draw(keys[8], (BANDS, TILE_COLS, NB, RMAX, TS), RMAX ** -0.5, 1.5, ((0, 16), (1, 16)), jnp.float32)
    right_factor = bell_draw(keys[9], (BANDS, TILE_COLS, NB, RMAX, TS), TS ** -0.5, 0.375, ((0, 16), (1, 16)), jnp.float32)
    return {"opening_old": opening_old, "pressure_old": pressure_old, "injection": injection, "front_flags": front_flags, "self_kernel": self_kernel, "source_column": source_column, "source_tile": source_tile, "source_rank": source_rank, "left_factor": left_factor, "right_factor": right_factor}


step_size = 0.1
highest_mode = lax.Precision.HIGHEST


def picard_pass(wide_open, wide_press, start_open, inject_part):
    row_count = wide_open.shape[0] - 2
    col_count = wide_open.shape[1] - 2
    cubed_open = wide_open * wide_open * wide_open

    def offset(array, shift_row, shift_col):
        return array[1 + shift_row:1 + shift_row + row_count, 1 + shift_col:1 + shift_col + col_count]

    cube_middle = offset(cubed_open, 0, 0)
    press_middle = offset(wide_press, 0, 0)
    accumulated = jnp.zeros_like(cube_middle)
    for shift_row, shift_col in ((1, 0), (-1, 0), (0, 1), (0, -1)):
        conduct = (cube_middle + offset(cubed_open, shift_row, shift_col)) / 24.0
        accumulated = accumulated + conduct * (offset(wide_press, shift_row, shift_col) - press_middle)
    return start_open + step_size * (accumulated + inject_part)


def reference(opening_old, pressure_old, injection, front_flags, self_kernel, source_column, source_tile, source_rank, left_factor, right_factor):
    current = opening_old
    wide_press = jnp.pad(pressure_old, 1)
    for passes_done in range(PASSES):
        current = picard_pass(jnp.pad(current, 1), wide_press, opening_old, injection)
    row_tiles = BR // TSIDE
    col_tiles = BC // TSIDE
    shaped = current.reshape(N_ROW, row_tiles, TSIDE, N_COL, col_tiles, TSIDE).transpose(0, 3, 1, 4, 2, 5)
    tile_rows = shaped.reshape(N_ROW, N_COL * T_DEV, TS) * front_flags[:, :, None].astype(jnp.float32)
    back = tile_rows.reshape(N_ROW, N_COL, row_tiles, col_tiles, TSIDE, TSIDE).transpose(0, 2, 4, 1, 3, 5)
    opening_new = back.reshape(N_ROW * BR, N_COL * BC)
    index = (source_column * T_DEV + source_tile).astype(jnp.int32).reshape(N_ROW, -1)
    sources = jnp.take_along_axis(tile_rows, index[:, :, None], axis=1).reshape(N_ROW, N_COL * T_DEV, NB, TS)
    rank_keep = (jnp.arange(RMAX)[None, None, None, :] < source_rank[:, :, :, None]).astype(jnp.float32)
    coefficients = jnp.einsum("rtkjs,rtks->rtkj", right_factor, sources, precision=highest_mode) * rank_keep
    near_terms = jnp.einsum("rtkjs,rtkj->rts", left_factor, coefficients, precision=highest_mode)
    self_terms = jnp.einsum("su,rtu->rts", self_kernel, tile_rows, precision=highest_mode)
    pressure_tiles = self_terms + near_terms
    laid = pressure_tiles.reshape(N_ROW, N_COL, row_tiles, col_tiles, TSIDE, TSIDE).transpose(0, 2, 4, 1, 3, 5)
    pressure_new = laid.reshape(N_ROW * BR, N_COL * BC)
    return opening_new, pressure_new
```

```python
import functools

import jax
import jax.numpy as jnp
from jax import lax
from jax.experimental import pallas as pl
from jax.experimental.pallas import tpu as pltpu
from jax.sharding import PartitionSpec as P

TSIDE = 16
PASSES = 3
STEP = 0.1
MESH = pl.DeviceIdType.MESH
F32 = jnp.float32
HIGHEST = lax.Precision.HIGHEST


def swap_blocks(parts):
    parts = list(parts)
    block = lax.broadcasted_iota(jnp.int32, (8, 128), 1) // TSIDE
    for bit in (1, 2, 4):
        upper = (block & bit) != 0
        for i in range(8):
            if i & bit:
                continue
            a, b = parts[i], parts[i + bit]
            parts[i] = jnp.where(upper, pltpu.roll(b, TSIDE * bit, 1), a)
            parts[i + bit] = jnp.where(upper, b, pltpu.roll(a, 128 - TSIDE * bit, 1))
    return parts


def split_bf16(x):
    high = x.astype(jnp.bfloat16)
    low = (x - high.astype(F32)).astype(jnp.bfloat16)
    return high, low


def kernel(
    rows, cols,
    opening_ref, pressure_ref, injection_ref, flags_ref, self_ref,
    column_ref, tile_ref, rank_ref, left_ref, right_ref,
    opening_out, pressure_out,
    field, turned, edge_rows, edge_cols, middle, band, left, right, self_kernel, flags, near,
    column, tile, rank,
    field_sem, small_sem, factor_sem, edge_send, edge_recv, band_send, band_recv,
):
    r, c = lax.axis_index("row"), lax.axis_index("col")
    north, south = lax.rem(r + rows - 1, rows), lax.rem(r + 1, rows)
    west, east = lax.rem(c + cols - 1, cols), lax.rem(c + 1, cols)
    neighbours = [(north, c), (south, c), (north, west), (north, east), (south, west), (south, east)]

    barrier = pltpu.get_barrier_semaphore()
    for target in neighbours:
        pl.semaphore_signal(barrier, inc=1, device_id=target, device_id_type=MESH)
    for step in range(1, cols):
        pl.semaphore_signal(
            barrier, inc=1, device_id=(r, lax.rem(c + step, cols)), device_id_type=MESH
        )

    field_copies = [
        pltpu.make_async_copy(ref, field.at[i], field_sem.at[i])
        for i, ref in enumerate((opening_ref, pressure_ref, injection_ref))
    ]
    small_copies = [
        pltpu.make_async_copy(ref, to, small_sem.at[i])
        for i, (ref, to) in enumerate(
            ((flags_ref, flags), (self_ref, self_kernel), (column_ref, column), (tile_ref, tile), (rank_ref, rank))
        )
    ]
    factor_copies = [
        pltpu.make_async_copy(right_ref, right, factor_sem.at[0]),
        pltpu.make_async_copy(left_ref, left, factor_sem.at[1]),
    ]
    for copy in field_copies + small_copies + factor_copies:
        copy.start()
    for copy in field_copies:
        copy.wait()
    for i in range(3):
        turned[i] = field[i].T
    edge_cols[:, pl.ds(8, 112), :] = jnp.zeros((3, 112, 128), F32)

    pl.semaphore_wait(barrier, len(neighbours) + cols - 1)

    top, bottom = pl.ds(0, 8), pl.ds(120, 8)
    sends = []

    def send(src, dst, slot, target):
        copy = pltpu.make_async_remote_copy(
            src_ref=src, dst_ref=dst, send_sem=edge_send.at[slot], recv_sem=edge_recv.at[slot],
            device_id=target, device_id_type=MESH,
        )
        copy.start()
        sends.append(copy)

    send(field.at[:, top, :], edge_rows.at[1], 1, (north, c))
    send(field.at[:, bottom, :], edge_rows.at[0], 0, (south, c))
    send(turned.at[:, top, :], edge_cols.at[:, top, :], 6, (r, west))
    send(turned.at[:, bottom, :], edge_cols.at[:, bottom, :], 7, (r, east))
    send(field.at[:, top, :], edge_rows.at[5], 5, (north, west))
    send(field.at[:, top, :], edge_rows.at[4], 4, (north, east))
    send(field.at[:, bottom, :], edge_rows.at[3], 3, (south, west))
    send(field.at[:, bottom, :], edge_rows.at[2], 2, (south, east))

    small_copies[0].wait()
    lane = lax.broadcasted_iota(jnp.int32, (8, 64), 1)
    sub = lax.broadcasted_iota(jnp.int32, (8, 64), 0)
    spread = jnp.where(lane // 8 == sub, flags[...].astype(F32), 0.0)
    from_tile = lax.broadcasted_iota(jnp.int32, (64, 128), 0)
    to_lane = lax.broadcasted_iota(jnp.int32, (64, 128), 1)
    inside = jnp.dot(
        spread, (from_tile % 8 == to_lane // TSIDE).astype(F32), preferred_element_type=F32
    )

    wide_rows, wide_cols = 136, 256
    at_row = lax.broadcasted_iota(jnp.int32, (wide_rows, wide_cols), 0)
    at_col = lax.broadcasted_iota(jnp.int32, (wide_rows, wide_cols), 1)
    low_row = jnp.where(r == rows - 1, 128, 132)
    high_row = jnp.where(r == 0, 136, 132)
    low_col = jnp.where(c == cols - 1, 128, 192)
    high_col = jnp.where(c == 0, 256, 192)
    valid = ((at_row < low_row) | (at_row >= high_row)) & ((at_col < low_col) | (at_col >= high_col))
    upper_half = lax.broadcasted_iota(jnp.int32, (8, 128), 0) < 4
    left_half = lax.broadcasted_iota(jnp.int32, (8, 128), 1) < 64

    for copy in sends:
        copy.wait_recv()

    wide = []
    for i in range(3):
        beside = edge_cols[i].T
        under = jnp.where(upper_half, edge_rows[1, i], edge_rows[0, i])
        corner = jnp.where(
            left_half,
            jnp.where(upper_half, edge_rows[5, i], edge_rows[3, i]),
            jnp.where(upper_half, edge_rows[4, i], edge_rows[2, i]),
        )
        whole = jnp.concatenate(
            [jnp.concatenate([field[i], beside], axis=1), jnp.concatenate([under, corner], axis=1)], axis=0
        )
        wide.append(jnp.where(valid, whole, 0.0))
    start, press, source = wide
    across = (pltpu.roll(press, wide_cols - 1, 1) - press) / 24.0
    down = (pltpu.roll(press, wide_rows - 1, 0) - press) / 24.0
    current = start
    for _ in range(PASSES):
        cubed = current * current * current
        flux_across = (cubed + pltpu.roll(cubed, wide_cols - 1, 1)) * across
        flux_down = (cubed + pltpu.roll(cubed, wide_rows - 1, 0)) * down
        total = (flux_across - pltpu.roll(flux_across, 1, 1)) + (flux_down - pltpu.roll(flux_down, 1, 0))
        current = jnp.where(valid, start + STEP * (total + source), 0.0)
    middle[...] = current[:128, :128]

    own = pl.multiple_of(c * 64, 64)
    rows_of = [middle[pl.ds(i, 8, stride=TSIDE), :] * inside for i in range(TSIDE)]
    for i in range(TSIDE):
        opening_out[pl.ds(i, 8, stride=TSIDE), :] = rows_of[i]
    first, second = swap_blocks(rows_of[:8]), swap_blocks(rows_of[8:])
    for e in range(8):
        near[0, pl.ds(e, 8, stride=8), :] = first[e]
        near[1, pl.ds(e, 8, stride=8), :] = second[e]
    tiles = jnp.concatenate([near[0], near[1]], axis=1)
    band[pl.ds(own, 64), :] = tiles

    band_sends = []
    for step in range(1, cols):
        copy = pltpu.make_async_remote_copy(
            src_ref=band.at[pl.ds(own, 64), :], dst_ref=band.at[pl.ds(own, 64), :],
            send_sem=band_send.at[step], recv_sem=band_recv.at[step],
            device_id=(r, lax.rem(c + step, cols)), device_id_type=MESH,
        )
        copy.start()
        band_sends.append(copy)

    small_copies[1].wait()
    own_term = lax.dot_general(
        tiles, self_kernel[...], (((1,), (1,)), ((), ())), precision=HIGHEST, preferred_element_type=F32
    )
    near[0], near[1] = own_term[:, :128], own_term[:, 128:]
    for copy in small_copies[2:]:
        copy.wait()
    for copy in factor_copies:
        copy.wait()

    at_rank = lax.broadcasted_iota(jnp.int32, (16, 256), 0)

    def cut(t, carry):
        for k in range(4):
            left[t, k] = jnp.where(at_rank < rank[k, t], left[t, k], 0.0)
        return carry

    lax.fori_loop(0, 64, cut, 0)
    for copy in sends:
        copy.wait_send()
    for copy in band_sends:
        copy.wait()

    ones = jnp.ones((256, 128), jnp.bfloat16)
    group = 8

    def interact(g, carry):
        highs, lows = [], []
        for u in range(group):
            t = g * group + u
            for k in range(4):
                at = column[k, t] * 64 + tile[k, t]
                product = right[t, k] * band[pl.ds(at, 1), :]
                high, low = split_bf16(product[:, :128] + product[:, 128:])
                highs.append(high)
                lows.append(low)
        parts = jnp.concatenate([jnp.concatenate(highs, axis=0), jnp.concatenate(lows, axis=0)], axis=1)
        coefficients = jnp.dot(parts, ones, preferred_element_type=F32)
        sums = [[], []]
        for u in range(group):
            t = g * group + u
            factor = left[t].reshape(64, 256)
            scale = coefficients[u * 64:(u + 1) * 64]
            for h in range(2):
                sums[h].append(jnp.sum(factor[:, h * 128:(h + 1) * 128] * scale, axis=0, keepdims=True))
        at = pl.ds(pl.multiple_of(g * group, group), group)
        for h in range(2):
            near[h, at, :] = near[h, at, :] + jnp.concatenate(sums[h], axis=0)
        return carry

    lax.fori_loop(0, 64 // group, interact, 0)

    laid = []
    for h in range(2):
        laid += swap_blocks([near[h, pl.ds(e, 8, stride=8), :] for e in range(8)])
    for i in range(TSIDE):
        pressure_out[pl.ds(i, 8, stride=TSIDE), :] = laid[i]


def local(
    opening_old, pressure_old, injection, front_flags, self_kernel,
    source_column, source_tile, source_rank, left_factor, right_factor,
):
    rows, cols = lax.axis_size("row"), lax.axis_size("col")
    anywhere = pl.BlockSpec(memory_space=pl.ANY)
    out = jax.ShapeDtypeStruct((128, 128), F32)
    lists = [a[0].T for a in (source_column, source_tile, source_rank)]
    dma = pltpu.SemaphoreType.DMA
    return pl.pallas_call(
        functools.partial(kernel, rows, cols),
        out_shape=(out, out),
        in_specs=[anywhere] * 10,
        out_specs=(pl.BlockSpec(memory_space=pltpu.VMEM),) * 2,
        scratch_shapes=[
            pltpu.VMEM((3, 128, 128), F32),
            pltpu.VMEM((3, 128, 128), F32),
            pltpu.VMEM((6, 3, 8, 128), F32),
            pltpu.VMEM((3, 128, 128), F32),
            pltpu.VMEM((128, 128), F32),
            pltpu.VMEM((64 * cols, 256), F32),
            pltpu.VMEM((64, 4, 16, 256), F32),
            pltpu.VMEM((64, 4, 16, 256), F32),
            pltpu.VMEM((256, 256), F32),
            pltpu.VMEM((1, 64), jnp.int32),
            pltpu.VMEM((2, 64, 128), F32),
            pltpu.SMEM((4, 64), jnp.int32),
            pltpu.SMEM((4, 64), jnp.int32),
            pltpu.SMEM((4, 64), jnp.int32),
            dma((3,)),
            dma((5,)),
            dma((2,)),
            dma((8,)),
            dma((8,)),
            dma((16,)),
            dma((16,)),
        ],
        compiler_params=pltpu.CompilerParams(
            collective_id=0, has_side_effects=True, vmem_limit_bytes=58 * 1024 * 1024
        ),
        name="fracture",
    )(opening_old, pressure_old, injection, front_flags, self_kernel, *lists, left_factor[0], right_factor[0])


def solution(mesh):
    fields, lists, factors = P("row", "col"), P("row", "col", None), P("row", "col", None, None, None)
    return jax.shard_map(
        local,
        mesh=mesh,
        in_specs=(fields, fields, fields, fields, P(), lists, lists, lists, factors, factors),
        out_specs=(fields, fields),
        check_vma=False,
    )
```

```python
import functools

import jax
import jax.numpy as jnp
from jax import lax
from jax.experimental import pallas as pl
from jax.experimental.pallas import tpu as pltpu
from jax.sharding import PartitionSpec as P

TSIDE = 16
PASSES = 3
STEP = 0.1
MESH = pl.DeviceIdType.MESH
F32 = jnp.float32
HIGHEST = lax.Precision.HIGHEST


def swap_blocks(parts):
    parts = list(parts)
    block = lax.broadcasted_iota(jnp.int32, (8, 128), 1) // TSIDE
    for bit in (1, 2, 4):
        upper = (block & bit) != 0
        for i in range(8):
            if i & bit:
                continue
            a, b = parts[i], parts[i + bit]
            parts[i] = jnp.where(upper, pltpu.roll(b, TSIDE * bit, 1), a)
            parts[i + bit] = jnp.where(upper, b, pltpu.roll(a, 128 - TSIDE * bit, 1))
    return parts


def split_bf16(x):
    high = x.astype(jnp.bfloat16)
    low = (x - high.astype(F32)).astype(jnp.bfloat16)
    return high, low


def flat_tiles(rows_of):
    return swap_blocks(rows_of[:8]), swap_blocks(rows_of[8:])


def kernel(
    rows, cols,
    opening_ref, pressure_ref, injection_ref, flags_ref, self_ref,
    column_ref, tile_ref, rank_ref, left_ref, right_ref,
    opening_out, pressure_out,
    field, turned, edge_rows, edge_cols, middle, early, band, patches, left, right, self_kernel, flags, near,
    column, tile, rank,
    field_sem, small_sem, factor_sem, edge_send, edge_recv, early_send, early_recv, pass_send, pass_recv,
    patch_send, patch_recv,
):
    r, c = lax.axis_index("row"), lax.axis_index("col")
    west, east = lax.rem(c + cols - 1, cols), lax.rem(c + 1, cols)
    has_north, has_south = r > 0, r < rows - 1
    north, south = jnp.maximum(r - 1, 0), jnp.minimum(r + 1, rows - 1)

    barrier = pltpu.get_barrier_semaphore()
    for there, to in ((has_north, north), (has_south, south)):
        @pl.when(there)
        def _():
            for beside in (c, west, east):
                pl.semaphore_signal(barrier, inc=1, device_id=(to, beside), device_id_type=MESH)
    for step in range(1, cols):
        pl.semaphore_signal(
            barrier, inc=1, device_id=(r, lax.rem(c + step, cols)), device_id_type=MESH
        )

    field_copies = [
        pltpu.make_async_copy(ref, field.at[i], field_sem.at[i])
        for i, ref in enumerate((opening_ref, pressure_ref, injection_ref))
    ]
    small_copies = [
        pltpu.make_async_copy(ref, to, small_sem.at[i])
        for i, (ref, to) in enumerate(
            ((flags_ref, flags), (self_ref, self_kernel), (column_ref, column), (tile_ref, tile), (rank_ref, rank))
        )
    ]
    factor_copies = [
        pltpu.make_async_copy(right_ref, right, factor_sem.at[0]),
        pltpu.make_async_copy(left_ref, left, factor_sem.at[1]),
    ]
    for copy in field_copies + small_copies + factor_copies:
        copy.start()
    for copy in field_copies:
        copy.wait()
    for i in range(3):
        turned[i] = field[i].T
    edge_cols[:, pl.ds(8, 112), :] = jnp.zeros((3, 112, 128), F32)

    sends, sends_north, sends_south = [], [], []
    top, bottom = pl.ds(0, 8), pl.ds(120, 8)

    def edge(src, dst, slot, target, to):
        to.append(pltpu.make_async_remote_copy(
            src_ref=src, dst_ref=dst, send_sem=edge_send.at[slot], recv_sem=edge_recv.at[slot],
            device_id=target, device_id_type=MESH,
        ))

    edge(field.at[:, top, :], edge_rows.at[1], 1, (north, c), sends_north)
    edge(field.at[:, top, :], edge_rows.at[5], 5, (north, west), sends_north)
    edge(field.at[:, top, :], edge_rows.at[4], 4, (north, east), sends_north)
    edge(field.at[:, bottom, :], edge_rows.at[0], 0, (south, c), sends_south)
    edge(field.at[:, bottom, :], edge_rows.at[3], 3, (south, west), sends_south)
    edge(field.at[:, bottom, :], edge_rows.at[2], 2, (south, east), sends_south)
    edge(turned.at[:, top, :], edge_cols.at[:, top, :], 6, (r, west), sends)
    edge(turned.at[:, bottom, :], edge_cols.at[:, bottom, :], 7, (r, east), sends)

    pl.semaphore_wait(
        barrier, 3 * has_north.astype(jnp.int32) + 3 * has_south.astype(jnp.int32) + cols - 1
    )

    for there, group in ((has_north, sends_north), (has_south, sends_south)):
        @pl.when(there)
        def _():
            for copy in group:
                copy.start()
    for copy in sends:
        copy.start()

    small_copies[0].wait()
    lane = lax.broadcasted_iota(jnp.int32, (8, 64), 1)
    sub = lax.broadcasted_iota(jnp.int32, (8, 64), 0)
    spread = jnp.where(lane // 8 == sub, flags[...].astype(F32), 0.0)
    from_tile = lax.broadcasted_iota(jnp.int32, (64, 128), 0)
    to_lane = lax.broadcasted_iota(jnp.int32, (64, 128), 1)
    inside = jnp.dot(
        spread, (from_tile % 8 == to_lane // TSIDE).astype(F32), preferred_element_type=F32
    )

    def passes(start, press, source, keep):
        height, width = start.shape
        across = (pltpu.roll(press, width - 1, 1) - press) / 24.0
        down = (pltpu.roll(press, height - 1, 0) - press) / 24.0
        current = start
        for _ in range(PASSES):
            cubed = current * current * current
            flux_across = (cubed + pltpu.roll(cubed, width - 1, 1)) * across
            flux_down = (cubed + pltpu.roll(cubed, height - 1, 0)) * down
            total = (flux_across - pltpu.roll(flux_across, 1, 1)) + (flux_down - pltpu.roll(flux_down, 1, 0))
            current = keep(start + STEP * (total + source))
        return current

    middle[...] = passes(field[0], field[1], field[2], lambda v: v)
    first, second = flat_tiles([middle[pl.ds(i, 8, stride=TSIDE), :] * inside for i in range(TSIDE)])
    for e in range(8):
        early[0, pl.ds(e, 8, stride=8), :] = first[e]
        early[1, pl.ds(e, 8, stride=8), :] = second[e]

    def block(of):
        return band.at[:, pl.ds(pl.multiple_of(of * 64, 64), 64), :]

    sibling = (r, c ^ 1)
    chips = (4, 5, 3, 7, 1, 2, 6)
    early_sends = [
        pltpu.make_async_remote_copy(
            src_ref=early, dst_ref=block(c), send_sem=early_send.at[i], recv_sem=early_recv.at[i],
            device_id=sibling if i == 0 else (r, c ^ (2 * i)), device_id_type=MESH,
        )
        for i in chips + (0,)
    ]
    for copy in early_sends:
        copy.start()

    wide_rows, wide_cols = 136, 256
    at_row = lax.broadcasted_iota(jnp.int32, (wide_rows, wide_cols), 0)
    at_col = lax.broadcasted_iota(jnp.int32, (wide_rows, wide_cols), 1)
    low_row = jnp.where(r == rows - 1, 128, 132)
    high_row = jnp.where(r == 0, 136, 132)
    low_col = jnp.where(c == cols - 1, 128, 192)
    high_col = jnp.where(c == 0, 256, 192)
    valid = ((at_row < low_row) | (at_row >= high_row)) & ((at_col < low_col) | (at_col >= high_col))
    upper_half = lax.broadcasted_iota(jnp.int32, (8, 128), 0) < 4
    left_half = lax.broadcasted_iota(jnp.int32, (8, 128), 1) < 64

    for there, group in ((has_south, sends_north), (has_north, sends_south)):
        @pl.when(there)
        def _():
            for copy in group:
                copy.wait_recv()
    for copy in sends:
        copy.wait_recv()

    wide = []
    for i in range(3):
        beside = edge_cols[i].T
        under = jnp.where(upper_half, edge_rows[1, i], edge_rows[0, i])
        corner = jnp.where(
            left_half,
            jnp.where(upper_half, edge_rows[5, i], edge_rows[3, i]),
            jnp.where(upper_half, edge_rows[4, i], edge_rows[2, i]),
        )
        whole = jnp.concatenate(
            [jnp.concatenate([field[i], beside], axis=1), jnp.concatenate([under, corner], axis=1)], axis=0
        )
        wide.append(jnp.where(valid, whole, 0.0))
    current = passes(*wide, lambda v: jnp.where(valid, v, 0.0))
    middle[...] = current[:128, :128]

    own = pl.multiple_of(c * 64, 64)
    rows_of = [middle[pl.ds(i, 8, stride=TSIDE), :] * inside for i in range(TSIDE)]
    first, second = flat_tiles(rows_of)
    for e in range(8):
        band[0, pl.ds(own + e, 8, stride=8), :] = first[e]
        band[1, pl.ds(own + e, 8, stride=8), :] = second[e]

    at_lane = lax.broadcasted_iota(jnp.int32, (8, 128), 1)
    in_row = at_lane % TSIDE
    left_edge, right_edge = in_row < PASSES, in_row >= TSIDE - PASSES
    outer = left_edge | right_edge
    ends = [jnp.where(in_row < TSIDE // 2, half[0], half[7]) for half in (first, second)]
    patches[c, 0] = jnp.where(outer, ends[0], pltpu.roll(ends[1], 6, 1))
    patches[c, 1] = jnp.where(
        left_half, band[0, pl.ds(own, 8), :], band[1, pl.ds(pl.multiple_of(own + 56, 8), 8), :]
    )
    patch_sends = []
    for step in range(1, cols):
        copy = pltpu.make_async_remote_copy(
            src_ref=patches.at[c], dst_ref=patches.at[c],
            send_sem=patch_send.at[step], recv_sem=patch_recv.at[step],
            device_id=(r, lax.rem(c + step, cols)), device_id_type=MESH,
        )
        copy.start()
        patch_sends.append(copy)
    for i in range(TSIDE):
        opening_out[pl.ds(i, 8, stride=TSIDE), :] = rows_of[i]

    passed = []
    for n, i in enumerate(chips):
        early_sends[n].wait_recv()
        copy = pltpu.make_async_remote_copy(
            src_ref=block(c ^ (2 * i)), dst_ref=block(c ^ (2 * i)),
            send_sem=pass_send.at[i], recv_sem=pass_recv.at[i],
            device_id=sibling, device_id_type=MESH,
        )
        copy.start()
        passed.append(copy)

    small_copies[1].wait()
    own_tiles = jnp.concatenate([band[h, pl.ds(own, 64), :] for h in range(2)], axis=1)
    own_term = lax.dot_general(
        own_tiles, self_kernel[...], (((1,), (1,)), ((), ())), precision=HIGHEST, preferred_element_type=F32
    )
    near[0], near[1] = own_term[:, :128], own_term[:, 128:]
    for copy in small_copies[2:]:
        copy.wait()
    for copy in factor_copies:
        copy.wait()

    at_rank = lax.broadcasted_iota(jnp.int32, (16, 256), 0)

    def cut(t, carry):
        for k in range(4):
            left[t, k] = jnp.where(at_rank < rank[k, t], left[t, k], 0.0)
        return carry

    lax.fori_loop(0, 64, cut, 0)
    for there, group in ((has_north, sends_north), (has_south, sends_south)):
        @pl.when(there)
        def _():
            for copy in group:
                copy.wait_send()
    for copy in sends + early_sends + patch_sends:
        copy.wait_send()
    early_sends[-1].wait_recv()
    for copy in passed:
        copy.wait()
    for copy in patch_sends:
        copy.wait_recv()

    def patch(step, carry):
        of = lax.rem(c + step, cols)
        base = pl.multiple_of(of * 64, 64)
        columns = patches[of, 0]
        for h, value in ((0, columns), (1, pltpu.roll(columns, 122, 1))):
            for start, mask in ((base, left_edge), (base + 7, right_edge)):
                at = pl.ds(start, 8, stride=8)
                band[h, at, :] = jnp.where(mask, value, band[h, at, :])
        for h, start, mask in (
            (0, base, at_lane < PASSES * TSIDE), (1, base + 56, at_lane >= 128 - PASSES * TSIDE)
        ):
            at = pl.ds(pl.multiple_of(start, 8), 8)
            band[h, at, :] = jnp.where(mask, patches[of, 1], band[h, at, :])
        return carry

    lax.fori_loop(1, cols, patch, 0)

    ones = jnp.ones((256, 128), jnp.bfloat16)
    group = 8

    def interact(g, carry):
        highs, lows = [], []
        for u in range(group):
            t = g * group + u
            for k in range(4):
                at = column[k, t] * 64 + tile[k, t]
                factor = right[t, k]
                high, low = split_bf16(
                    factor[:, :128] * band[0, pl.ds(at, 1), :] + factor[:, 128:] * band[1, pl.ds(at, 1), :]
                )
                highs.append(high)
                lows.append(low)
        parts = jnp.concatenate([jnp.concatenate(highs, axis=0), jnp.concatenate(lows, axis=0)], axis=1)
        coefficients = jnp.dot(parts, ones, preferred_element_type=F32)
        sums = [[], []]
        for u in range(group):
            t = g * group + u
            factor = left[t].reshape(64, 256)
            scale = coefficients[u * 64:(u + 1) * 64]
            for h in range(2):
                sums[h].append(jnp.sum(factor[:, h * 128:(h + 1) * 128] * scale, axis=0, keepdims=True))
        at = pl.ds(pl.multiple_of(g * group, group), group)
        for h in range(2):
            near[h, at, :] = near[h, at, :] + jnp.concatenate(sums[h], axis=0)
        return carry

    lax.fori_loop(0, 64 // group, interact, 0)

    laid = []
    for h in range(2):
        laid += swap_blocks([near[h, pl.ds(e, 8, stride=8), :] for e in range(8)])
    for i in range(TSIDE):
        pressure_out[pl.ds(i, 8, stride=TSIDE), :] = laid[i]


def local(
    opening_old, pressure_old, injection, front_flags, self_kernel,
    source_column, source_tile, source_rank, left_factor, right_factor,
):
    rows, cols = lax.axis_size("row"), lax.axis_size("col")
    anywhere = pl.BlockSpec(memory_space=pl.ANY)
    out = jax.ShapeDtypeStruct((128, 128), F32)
    lists = [a[0].T for a in (source_column, source_tile, source_rank)]
    dma = pltpu.SemaphoreType.DMA
    return pl.pallas_call(
        functools.partial(kernel, rows, cols),
        out_shape=(out, out),
        in_specs=[anywhere] * 10,
        out_specs=(pl.BlockSpec(memory_space=pltpu.VMEM),) * 2,
        scratch_shapes=[
            pltpu.VMEM((3, 128, 128), F32),
            pltpu.VMEM((3, 128, 128), F32),
            pltpu.VMEM((6, 3, 8, 128), F32),
            pltpu.VMEM((3, 128, 128), F32),
            pltpu.VMEM((128, 128), F32),
            pltpu.VMEM((2, 64, 128), F32),
            pltpu.VMEM((2, 64 * cols, 128), F32),
            pltpu.VMEM((cols, 2, 8, 128), F32),
            pltpu.VMEM((64, 4, 16, 256), F32),
            pltpu.VMEM((64, 4, 16, 256), F32),
            pltpu.VMEM((256, 256), F32),
            pltpu.VMEM((1, 64), jnp.int32),
            pltpu.VMEM((2, 64, 128), F32),
            pltpu.SMEM((4, 64), jnp.int32),
            pltpu.SMEM((4, 64), jnp.int32),
            pltpu.SMEM((4, 64), jnp.int32),
            dma((3,)),
            dma((5,)),
            dma((2,)),
            dma((8,)),
            dma((8,)),
            dma((8,)),
            dma((8,)),
            dma((8,)),
            dma((8,)),
            dma((16,)),
            dma((16,)),
        ],
        compiler_params=pltpu.CompilerParams(
            collective_id=0, has_side_effects=True, vmem_limit_bytes=58 * 1024 * 1024
        ),
        name="fracture",
    )(opening_old, pressure_old, injection, front_flags, self_kernel, *lists, left_factor[0], right_factor[0])


def solution(mesh):
    fields, lists, factors = P("row", "col"), P("row", "col", None), P("row", "col", None, None, None)
    return jax.shard_map(
        local,
        mesh=mesh,
        in_specs=(fields, fields, fields, fields, P(), lists, lists, lists, factors, factors),
        out_specs=(fields, fields),
        check_vma=False,
    )
```

```python
import functools

import jax
import jax.numpy as jnp
from jax import lax
from jax.experimental import pallas as pl
from jax.experimental.pallas import tpu as pltpu
from jax.sharding import PartitionSpec as P

TSIDE = 16
PASSES = 3
STEP = 0.1
MESH = pl.DeviceIdType.MESH
F32 = jnp.float32
HIGHEST = lax.Precision.HIGHEST


def swap_blocks(parts):
    parts = list(parts)
    block = lax.broadcasted_iota(jnp.int32, (8, 128), 1) // TSIDE
    for bit in (1, 2, 4):
        upper = (block & bit) != 0
        for i in range(8):
            if i & bit:
                continue
            a, b = parts[i], parts[i + bit]
            parts[i] = jnp.where(upper, pltpu.roll(b, TSIDE * bit, 1), a)
            parts[i + bit] = jnp.where(upper, b, pltpu.roll(a, 128 - TSIDE * bit, 1))
    return parts


def split_bf16(x):
    high = x.astype(jnp.bfloat16)
    low = (x - high.astype(F32)).astype(jnp.bfloat16)
    return high, low


def flat_tiles(rows_of):
    return swap_blocks(rows_of[:8]), swap_blocks(rows_of[8:])


def kernel(
    rows, cols,
    opening_ref, pressure_ref, injection_ref, flags_ref, self_ref,
    column_ref, tile_ref, rank_ref, left_ref, right_ref,
    opening_out, pressure_out,
    field, turned, from_side, edge_rows, edge_cols, middle, early, band, patches, left, right, self_kernel, flags, near,
    column, tile, rank,
    field_sem, small_sem, factor_sem, edge_send, edge_recv, early_send, early_recv, pass_send, pass_recv,
    patch_send, patch_recv,
):
    r, c = lax.axis_index("row"), lax.axis_index("col")
    west, east = lax.rem(c + cols - 1, cols), lax.rem(c + 1, cols)
    has_north, has_south = r > 0, r < rows - 1
    north, south = jnp.maximum(r - 1, 0), jnp.minimum(r + 1, rows - 1)

    field_copies = [
        pltpu.make_async_copy(ref, field.at[i], field_sem.at[i])
        for i, ref in enumerate((opening_ref, pressure_ref, injection_ref))
    ]
    small_copies = [
        pltpu.make_async_copy(ref, to, small_sem.at[i])
        for i, (ref, to) in enumerate(
            ((flags_ref, flags), (self_ref, self_kernel), (column_ref, column), (tile_ref, tile), (rank_ref, rank))
        )
    ]
    factor_copies = [
        pltpu.make_async_copy(right_ref, right, factor_sem.at[0]),
        pltpu.make_async_copy(left_ref, left, factor_sem.at[1]),
    ]
    for copy in field_copies + small_copies:
        copy.start()

    barrier = pltpu.get_barrier_semaphore()
    for there, to in ((has_north, north), (has_south, south)):
        @pl.when(there)
        def _():
            for beside in (c, west, east):
                pl.semaphore_signal(barrier, inc=1, device_id=(to, beside), device_id_type=MESH)
    for step in range(1, cols):
        pl.semaphore_signal(
            barrier, inc=1, device_id=(r, lax.rem(c + step, cols)), device_id_type=MESH
        )

    for copy in field_copies:
        copy.wait()
    for i in range(3):
        turned[i] = field[i].T
    edge_cols[:, pl.ds(8, 112), :] = jnp.zeros((3, 112, 128), F32)

    sends, sends_north, sends_south = [], [], []
    top, bottom = pl.ds(0, 8), pl.ds(120, 8)

    def edge(src, dst, slot, target, to):
        to.append(pltpu.make_async_remote_copy(
            src_ref=src, dst_ref=dst, send_sem=edge_send.at[slot], recv_sem=edge_recv.at[slot],
            device_id=target, device_id_type=MESH,
        ))

    edge(field.at[:, top, :], edge_rows.at[5], 5, (north, west), sends_north)
    edge(field.at[:, top, :], edge_rows.at[4], 4, (north, east), sends_north)
    edge(field.at[:, top, :], edge_rows.at[1], 1, (north, c), sends_north)
    edge(field.at[:, bottom, :], edge_rows.at[3], 3, (south, west), sends_south)
    edge(field.at[:, bottom, :], edge_rows.at[2], 2, (south, east), sends_south)
    edge(field.at[:, bottom, :], edge_rows.at[0], 0, (south, c), sends_south)
    edge(turned.at[:, top, :], edge_cols.at[:, top, :], 6, (r, west), sends)
    edge(turned.at[:, bottom, :], edge_cols.at[:, bottom, :], 7, (r, east), sends)

    pl.semaphore_wait(
        barrier, 3 * has_north.astype(jnp.int32) + 3 * has_south.astype(jnp.int32) + cols - 1
    )

    for there, group in ((has_north, sends_north), (has_south, sends_south)):
        @pl.when(there)
        def _():
            for copy in group:
                copy.start()
    for copy in sends:
        copy.start()

    small_copies[0].wait()
    lane = lax.broadcasted_iota(jnp.int32, (8, 64), 1)
    sub = lax.broadcasted_iota(jnp.int32, (8, 64), 0)
    spread = jnp.where(lane // 8 == sub, flags[...].astype(F32), 0.0)
    from_tile = lax.broadcasted_iota(jnp.int32, (64, 128), 0)
    to_lane = lax.broadcasted_iota(jnp.int32, (64, 128), 1)
    inside = jnp.dot(
        spread, (from_tile % 8 == to_lane // TSIDE).astype(F32), preferred_element_type=F32
    )

    def passes(start, press, source, keep):
        height, width = start.shape
        across = (pltpu.roll(press, width - 1, 1) - press) / 24.0
        down = (pltpu.roll(press, height - 1, 0) - press) / 24.0
        current = start
        for _ in range(PASSES):
            cubed = current * current * current
            flux_across = (cubed + pltpu.roll(cubed, width - 1, 1)) * across
            flux_down = (cubed + pltpu.roll(cubed, height - 1, 0)) * down
            total = (flux_across - pltpu.roll(flux_across, 1, 1)) + (flux_down - pltpu.roll(flux_down, 1, 0))
            current = keep(start + STEP * (total + source))
        return current

    middle[...] = passes(field[0], field[1], field[2], lambda v: v)
    first, second = flat_tiles([middle[pl.ds(i, 8, stride=TSIDE), :] * inside for i in range(TSIDE)])
    for e in range(8):
        early[0, pl.ds(e, 8, stride=8), :] = first[e]
        early[1, pl.ds(e, 8, stride=8), :] = second[e]

    def block(of):
        return band.at[:, pl.ds(pl.multiple_of(of * 64, 64), 64), :]

    sibling = (r, c ^ 1)
    chips = (4, 5, 3, 7, 1, 2, 6)
    early_sends = [
        pltpu.make_async_remote_copy(
            src_ref=early, dst_ref=block(c), send_sem=early_send.at[i], recv_sem=early_recv.at[i],
            device_id=sibling if i == 0 else (r, c ^ (2 * i)), device_id_type=MESH,
        )
        for i in chips + (0,)
    ]
    for copy in early_sends + factor_copies:
        copy.start()

    wide_rows, wide_cols = 136, 256
    at_row = lax.broadcasted_iota(jnp.int32, (wide_rows, wide_cols), 0)
    at_col = lax.broadcasted_iota(jnp.int32, (wide_rows, wide_cols), 1)
    low_row = jnp.where(r == rows - 1, 128, 132)
    high_row = jnp.where(r == 0, 136, 132)
    low_col = jnp.where(c == cols - 1, 128, 192)
    high_col = jnp.where(c == 0, 256, 192)
    valid = ((at_row < low_row) | (at_row >= high_row)) & ((at_col < low_col) | (at_col >= high_col))
    upper_half = lax.broadcasted_iota(jnp.int32, (8, 128), 0) < 4
    left_half = lax.broadcasted_iota(jnp.int32, (8, 128), 1) < 64

    for copy in sends:
        copy.wait_recv()
    for i in range(3):
        from_side[i] = edge_cols[i].T
    for there, group in ((has_south, sends_north), (has_north, sends_south)):
        @pl.when(there)
        def _():
            for copy in group:
                copy.wait_recv()
    wide = []
    for i in range(3):
        under = jnp.where(upper_half, edge_rows[1, i], edge_rows[0, i])
        corner = jnp.where(
            left_half,
            jnp.where(upper_half, edge_rows[5, i], edge_rows[3, i]),
            jnp.where(upper_half, edge_rows[4, i], edge_rows[2, i]),
        )
        whole = jnp.concatenate(
            [jnp.concatenate([field[i], from_side[i]], axis=1), jnp.concatenate([under, corner], axis=1)], axis=0
        )
        wide.append(jnp.where(valid, whole, 0.0))
    current = passes(*wide, lambda v: jnp.where(valid, v, 0.0))
    middle[...] = current[:128, :128]

    own = pl.multiple_of(c * 64, 64)
    rows_of = [middle[pl.ds(i, 8, stride=TSIDE), :] * inside for i in range(TSIDE)]
    first, second = flat_tiles(rows_of)
    for e in range(8):
        band[0, pl.ds(own + e, 8, stride=8), :] = first[e]
        band[1, pl.ds(own + e, 8, stride=8), :] = second[e]

    at_lane = lax.broadcasted_iota(jnp.int32, (8, 128), 1)
    in_row = at_lane % TSIDE
    left_edge, right_edge = in_row < PASSES, in_row >= TSIDE - PASSES
    outer = left_edge | right_edge
    ends = [jnp.where(in_row < TSIDE // 2, half[0], half[7]) for half in (first, second)]
    patches[c, 0] = jnp.where(outer, ends[0], pltpu.roll(ends[1], 6, 1))
    patches[c, 1] = jnp.where(
        left_half, band[0, pl.ds(own, 8), :], band[1, pl.ds(pl.multiple_of(own + 56, 8), 8), :]
    )
    patch_sends = []
    for step in (10, 11, 6, 7, 14, 15, 8, 9, 4, 5, 12, 13, 2, 3, 1):
        copy = pltpu.make_async_remote_copy(
            src_ref=patches.at[c], dst_ref=patches.at[c],
            send_sem=patch_send.at[step], recv_sem=patch_recv.at[step],
            device_id=(r, c ^ step), device_id_type=MESH,
        )
        copy.start()
        patch_sends.append(copy)
    for i in range(TSIDE):
        opening_out[pl.ds(i, 8, stride=TSIDE), :] = rows_of[i]

    passed = []
    for n, i in enumerate(chips):
        early_sends[n].wait_recv()
        copy = pltpu.make_async_remote_copy(
            src_ref=block(c ^ (2 * i)), dst_ref=block(c ^ (2 * i)),
            send_sem=pass_send.at[i], recv_sem=pass_recv.at[i],
            device_id=sibling, device_id_type=MESH,
        )
        copy.start()
        passed.append(copy)

    small_copies[1].wait()
    own_tiles = jnp.concatenate([band[h, pl.ds(own, 64), :] for h in range(2)], axis=1)
    own_term = lax.dot_general(
        own_tiles, self_kernel[...], (((1,), (1,)), ((), ())), precision=HIGHEST, preferred_element_type=F32
    )
    near[0], near[1] = own_term[:, :128], own_term[:, 128:]
    for copy in small_copies[2:]:
        copy.wait()
    for copy in factor_copies:
        copy.wait()

    at_rank = lax.broadcasted_iota(jnp.int32, (16, 256), 0)

    def cut(t, carry):
        for k in range(4):
            left[t, k] = jnp.where(at_rank < rank[k, t], left[t, k], 0.0)
        return carry

    lax.fori_loop(0, 64, cut, 0)
    for there, group in ((has_north, sends_north), (has_south, sends_south)):
        @pl.when(there)
        def _():
            for copy in group:
                copy.wait_send()
    for copy in sends + early_sends + patch_sends:
        copy.wait_send()
    early_sends[-1].wait_recv()
    for copy in passed:
        copy.wait()
    for copy in patch_sends:
        copy.wait_recv()

    def patch(step, carry):
        of = lax.rem(c + step, cols)
        base = pl.multiple_of(of * 64, 64)
        columns = patches[of, 0]
        for h, value in ((0, columns), (1, pltpu.roll(columns, 122, 1))):
            for start, mask in ((base, left_edge), (base + 7, right_edge)):
                at = pl.ds(start, 8, stride=8)
                band[h, at, :] = jnp.where(mask, value, band[h, at, :])
        for h, start, mask in (
            (0, base, at_lane < PASSES * TSIDE), (1, base + 56, at_lane >= 128 - PASSES * TSIDE)
        ):
            at = pl.ds(pl.multiple_of(start, 8), 8)
            band[h, at, :] = jnp.where(mask, patches[of, 1], band[h, at, :])
        return carry

    lax.fori_loop(1, cols, patch, 0)

    ones = jnp.ones((256, 128), jnp.bfloat16)
    group = 32

    def interact(g, carry):
        highs, lows = [], []
        for u in range(group):
            t = g * group + u
            for k in range(4):
                at = column[k, t] * 64 + tile[k, t]
                factor = right[t, k]
                high, low = split_bf16(
                    factor[:, :128] * band[0, pl.ds(at, 1), :] + factor[:, 128:] * band[1, pl.ds(at, 1), :]
                )
                highs.append(high)
                lows.append(low)
        parts = jnp.concatenate([jnp.concatenate(highs, axis=0), jnp.concatenate(lows, axis=0)], axis=1)
        coefficients = jnp.dot(parts, ones, preferred_element_type=F32)
        sums = [[], []]
        for u in range(group):
            t = g * group + u
            factor = left[t].reshape(64, 256)
            scale = coefficients[u * 64:(u + 1) * 64]
            for h in range(2):
                sums[h].append(jnp.sum(factor[:, h * 128:(h + 1) * 128] * scale, axis=0, keepdims=True))
        at = pl.ds(pl.multiple_of(g * group, group), group)
        for h in range(2):
            near[h, at, :] = near[h, at, :] + jnp.concatenate(sums[h], axis=0)
        return carry

    lax.fori_loop(0, 64 // group, interact, 0)

    laid = []
    for h in range(2):
        laid += swap_blocks([near[h, pl.ds(e, 8, stride=8), :] for e in range(8)])
    for i in range(TSIDE):
        pressure_out[pl.ds(i, 8, stride=TSIDE), :] = laid[i]


def local(
    opening_old, pressure_old, injection, front_flags, self_kernel,
    source_column, source_tile, source_rank, left_factor, right_factor,
):
    rows, cols = lax.axis_size("row"), lax.axis_size("col")
    anywhere = pl.BlockSpec(memory_space=pl.ANY)
    out = jax.ShapeDtypeStruct((128, 128), F32)
    lists = [a[0].T for a in (source_column, source_tile, source_rank)]
    operands = (opening_old, pressure_old, injection, front_flags, self_kernel, *lists, left_factor[0], right_factor[0])
    dma = pltpu.SemaphoreType.DMA
    return pl.pallas_call(
        functools.partial(kernel, rows, cols),
        out_shape=(out, out),
        in_specs=[anywhere] * 10,
        out_specs=(pl.BlockSpec(memory_space=pltpu.VMEM),) * 2,
        scratch_shapes=[
            pltpu.VMEM((3, 128, 128), F32),
            pltpu.VMEM((3, 128, 128), F32),
            pltpu.VMEM((3, 128, 128), F32),
            pltpu.VMEM((6, 3, 8, 128), F32),
            pltpu.VMEM((3, 128, 128), F32),
            pltpu.VMEM((128, 128), F32),
            pltpu.VMEM((2, 64, 128), F32),
            pltpu.VMEM((2, 64 * cols, 128), F32),
            pltpu.VMEM((cols, 2, 8, 128), F32),
            pltpu.VMEM((64, 4, 16, 256), F32),
            pltpu.VMEM((64, 4, 16, 256), F32),
            pltpu.VMEM((256, 256), F32),
            pltpu.VMEM((1, 64), jnp.int32),
            pltpu.VMEM((2, 64, 128), F32),
            pltpu.SMEM((4, 64), jnp.int32),
            pltpu.SMEM((4, 64), jnp.int32),
            pltpu.SMEM((4, 64), jnp.int32),
            dma((3,)),
            dma((5,)),
            dma((2,)),
            dma((8,)),
            dma((8,)),
            dma((8,)),
            dma((8,)),
            dma((8,)),
            dma((8,)),
            dma((16,)),
            dma((16,)),
        ],
        compiler_params=pltpu.CompilerParams(
            collective_id=0, has_side_effects=True, vmem_limit_bytes=40 * 1024 * 1024
        ),
        name="fracture",
    )(*[pltpu.with_memory_space_constraint(a, pltpu.HBM) for a in operands])


def solution(mesh):
    fields, lists, factors = P("row", "col"), P("row", "col", None), P("row", "col", None, None, None)
    return jax.shard_map(
        local,
        mesh=mesh,
        in_specs=(fields, fields, fields, fields, P(), lists, lists, lists, factors, factors),
        out_specs=(fields, fields),
        check_vma=False,
    )
```

```python
import functools

import jax
import jax.numpy as jnp
from jax import lax
from jax.experimental import pallas as pl
from jax.experimental.pallas import tpu as pltpu
from jax.sharding import PartitionSpec as P

TSIDE = 16
PASSES = 3
STEP = 0.1
MESH = pl.DeviceIdType.MESH
F32 = jnp.float32
HIGHEST = lax.Precision.HIGHEST


def swap_blocks(parts):
    parts = list(parts)
    block = lax.broadcasted_iota(jnp.int32, (8, 128), 1) // TSIDE
    for bit in (1, 2, 4):
        upper = (block & bit) != 0
        for i in range(8):
            if i & bit:
                continue
            a, b = parts[i], parts[i + bit]
            parts[i] = jnp.where(upper, pltpu.roll(b, TSIDE * bit, 1), a)
            parts[i + bit] = jnp.where(upper, b, pltpu.roll(a, 128 - TSIDE * bit, 1))
    return parts


def split_bf16(x):
    high = x.astype(jnp.bfloat16)
    low = (x - high.astype(F32)).astype(jnp.bfloat16)
    return high, low


def flat_tiles(rows_of):
    return swap_blocks(rows_of[:8]), swap_blocks(rows_of[8:])


def kernel(
    rows, cols,
    opening_ref, pressure_ref, injection_ref, flags_ref, self_ref,
    column_ref, tile_ref, rank_ref, left_ref, right_ref,
    opening_out, pressure_out,
    field, turned, from_side, edge_rows, edge_cols, middle, early, band, patches, left, right, self_kernel, flags, near,
    column, tile, rank,
    field_sem, small_sem, factor_sem, edge_send, edge_recv, early_send, early_recv, pass_send, pass_recv,
    patch_send, patch_recv,
):
    r, c = lax.axis_index("row"), lax.axis_index("col")
    west, east = lax.rem(c + cols - 1, cols), lax.rem(c + 1, cols)
    has_north, has_south = r > 0, r < rows - 1
    north, south = jnp.maximum(r - 1, 0), jnp.minimum(r + 1, rows - 1)

    field_copies = [
        pltpu.make_async_copy(ref, field.at[i], field_sem.at[i])
        for i, ref in enumerate((opening_ref, pressure_ref, injection_ref))
    ]
    small_copies = [
        pltpu.make_async_copy(ref, to, small_sem.at[i])
        for i, (ref, to) in enumerate(
            ((flags_ref, flags), (self_ref, self_kernel), (column_ref, column), (tile_ref, tile), (rank_ref, rank))
        )
    ]
    factor_copies = [
        pltpu.make_async_copy(right_ref, right, factor_sem.at[0]),
        pltpu.make_async_copy(left_ref, left, factor_sem.at[1]),
    ]
    for copy in field_copies + small_copies:
        copy.start()

    barrier = pltpu.get_barrier_semaphore()
    for there, to in ((has_north, north), (has_south, south)):
        @pl.when(there)
        def _():
            for beside in (c, west, east):
                pl.semaphore_signal(barrier, inc=1, device_id=(to, beside), device_id_type=MESH)
    for step in range(1, cols):
        pl.semaphore_signal(
            barrier, inc=1, device_id=(r, lax.rem(c + step, cols)), device_id_type=MESH
        )

    for copy in field_copies:
        copy.wait()
    for i in range(3):
        turned[i] = field[i].T
    edge_cols[:, pl.ds(8, 112), :] = jnp.zeros((3, 112, 128), F32)

    sends, sends_north, sends_south = [], [], []
    top, bottom = pl.ds(0, 8), pl.ds(120, 8)

    def edge(src, dst, slot, target, to):
        to.append(pltpu.make_async_remote_copy(
            src_ref=src, dst_ref=dst, send_sem=edge_send.at[slot], recv_sem=edge_recv.at[slot],
            device_id=target, device_id_type=MESH,
        ))

    edge(field.at[:, top, :], edge_rows.at[5], 5, (north, west), sends_north)
    edge(field.at[:, top, :], edge_rows.at[4], 4, (north, east), sends_north)
    edge(field.at[:, top, :], edge_rows.at[1], 1, (north, c), sends_north)
    edge(field.at[:, bottom, :], edge_rows.at[3], 3, (south, west), sends_south)
    edge(field.at[:, bottom, :], edge_rows.at[2], 2, (south, east), sends_south)
    edge(field.at[:, bottom, :], edge_rows.at[0], 0, (south, c), sends_south)
    edge(turned.at[:, top, :], edge_cols.at[:, top, :], 6, (r, west), sends)
    edge(turned.at[:, bottom, :], edge_cols.at[:, bottom, :], 7, (r, east), sends)

    pl.semaphore_wait(
        barrier, 3 * has_north.astype(jnp.int32) + 3 * has_south.astype(jnp.int32) + cols - 1
    )

    for there, group in ((has_north, sends_north), (has_south, sends_south)):
        @pl.when(there)
        def _():
            for copy in group:
                copy.start()
    for copy in sends:
        copy.start()

    small_copies[0].wait()
    lane = lax.broadcasted_iota(jnp.int32, (8, 64), 1)
    sub = lax.broadcasted_iota(jnp.int32, (8, 64), 0)
    spread = jnp.where(lane // 8 == sub, flags[...].astype(F32), 0.0)
    from_tile = lax.broadcasted_iota(jnp.int32, (64, 128), 0)
    to_lane = lax.broadcasted_iota(jnp.int32, (64, 128), 1)
    inside = jnp.dot(
        spread, (from_tile % 8 == to_lane // TSIDE).astype(F32), preferred_element_type=F32
    )

    def passes(start, press, source, keep):
        height, width = start.shape
        across = (pltpu.roll(press, width - 1, 1) - press) / 24.0
        down = (pltpu.roll(press, height - 1, 0) - press) / 24.0
        current = start
        for _ in range(PASSES):
            cubed = current * current * current
            flux_across = (cubed + pltpu.roll(cubed, width - 1, 1)) * across
            flux_down = (cubed + pltpu.roll(cubed, height - 1, 0)) * down
            total = (flux_across - pltpu.roll(flux_across, 1, 1)) + (flux_down - pltpu.roll(flux_down, 1, 0))
            current = keep(start + STEP * (total + source))
        return current

    middle[...] = passes(field[0], field[1], field[2], lambda v: v)
    first, second = flat_tiles([middle[pl.ds(i, 8, stride=TSIDE), :] * inside for i in range(TSIDE)])
    for e in range(8):
        early[0, pl.ds(e, 8, stride=8), :] = first[e]
        early[1, pl.ds(e, 8, stride=8), :] = second[e]

    def block(of):
        return band.at[:, pl.ds(pl.multiple_of(of * 64, 64), 64), :]

    sibling = (r, c ^ 1)
    chips = (4, 5, 3, 7, 1, 2, 6)
    early_sends = [
        pltpu.make_async_remote_copy(
            src_ref=early, dst_ref=block(c), send_sem=early_send.at[i], recv_sem=early_recv.at[i],
            device_id=sibling if i == 0 else (r, c ^ (2 * i)), device_id_type=MESH,
        )
        for i in chips + (0,)
    ]
    for copy in early_sends + factor_copies:
        copy.start()

    wide_rows, wide_cols = 136, 256
    at_row = lax.broadcasted_iota(jnp.int32, (wide_rows, wide_cols), 0)
    at_col = lax.broadcasted_iota(jnp.int32, (wide_rows, wide_cols), 1)
    low_row = jnp.where(r == rows - 1, 128, 132)
    high_row = jnp.where(r == 0, 136, 132)
    low_col = jnp.where(c == cols - 1, 128, 192)
    high_col = jnp.where(c == 0, 256, 192)
    valid = ((at_row < low_row) | (at_row >= high_row)) & ((at_col < low_col) | (at_col >= high_col))
    upper_half = lax.broadcasted_iota(jnp.int32, (8, 128), 0) < 4
    left_half = lax.broadcasted_iota(jnp.int32, (8, 128), 1) < 64

    for copy in sends:
        copy.wait_recv()
    for i in range(3):
        from_side[i] = edge_cols[i].T
    for there, group in ((has_south, sends_north), (has_north, sends_south)):
        @pl.when(there)
        def _():
            for copy in group:
                copy.wait_recv()
    wide = []
    for i in range(3):
        under = jnp.where(upper_half, edge_rows[1, i], edge_rows[0, i])
        corner = jnp.where(
            left_half,
            jnp.where(upper_half, edge_rows[5, i], edge_rows[3, i]),
            jnp.where(upper_half, edge_rows[4, i], edge_rows[2, i]),
        )
        whole = jnp.concatenate(
            [jnp.concatenate([field[i], from_side[i]], axis=1), jnp.concatenate([under, corner], axis=1)], axis=0
        )
        wide.append(jnp.where(valid, whole, 0.0))
    current = passes(*wide, lambda v: jnp.where(valid, v, 0.0))
    middle[...] = current[:128, :128]

    own = pl.multiple_of(c * 64, 64)
    rows_of = [middle[pl.ds(i, 8, stride=TSIDE), :] * inside for i in range(TSIDE)]
    first, second = flat_tiles(rows_of)
    for e in range(8):
        band[0, pl.ds(own + e, 8, stride=8), :] = first[e]
        band[1, pl.ds(own + e, 8, stride=8), :] = second[e]

    at_lane = lax.broadcasted_iota(jnp.int32, (8, 128), 1)
    in_row = at_lane % TSIDE
    left_edge, right_edge = in_row < PASSES, in_row >= TSIDE - PASSES
    outer = left_edge | right_edge
    ends = [jnp.where(in_row < TSIDE // 2, half[0], half[7]) for half in (first, second)]
    patches[c, 0] = jnp.where(outer, ends[0], pltpu.roll(ends[1], 6, 1))
    patches[c, 1] = jnp.where(
        left_half, band[0, pl.ds(own, 8), :], band[1, pl.ds(pl.multiple_of(own + 56, 8), 8), :]
    )
    patch_sends = []
    for step in (10, 11, 6, 7, 14, 15, 8, 9, 4, 5, 12, 13, 2, 3, 1):
        copy = pltpu.make_async_remote_copy(
            src_ref=patches.at[c], dst_ref=patches.at[c],
            send_sem=patch_send.at[step], recv_sem=patch_recv.at[step],
            device_id=(r, c ^ step), device_id_type=MESH,
        )
        copy.start()
        patch_sends.append(copy)
    for i in range(TSIDE):
        opening_out[pl.ds(i, 8, stride=TSIDE), :] = rows_of[i]

    passed = []
    for n, i in enumerate(chips):
        early_sends[n].wait_recv()
        copy = pltpu.make_async_remote_copy(
            src_ref=block(c ^ (2 * i)), dst_ref=block(c ^ (2 * i)),
            send_sem=pass_send.at[i], recv_sem=pass_recv.at[i],
            device_id=sibling, device_id_type=MESH,
        )
        copy.start()
        passed.append(copy)

    small_copies[1].wait()
    own_tiles = jnp.concatenate([band[h, pl.ds(own, 64), :] for h in range(2)], axis=1)
    own_term = lax.dot_general(
        own_tiles, self_kernel[...], (((1,), (1,)), ((), ())), precision=HIGHEST, preferred_element_type=F32
    )
    near[0], near[1] = own_term[:, :128], own_term[:, 128:]
    for copy in small_copies[2:]:
        copy.wait()
    for copy in factor_copies:
        copy.wait()

    at_rank = lax.broadcasted_iota(jnp.int32, (16, 256), 0)

    def cut(t, carry):
        for k in range(4):
            left[t, k] = jnp.where(at_rank < rank[k, t], left[t, k], 0.0)
        return carry

    lax.fori_loop(0, 64, cut, 0)
    for there, group in ((has_north, sends_north), (has_south, sends_south)):
        @pl.when(there)
        def _():
            for copy in group:
                copy.wait_send()
    for copy in sends + early_sends + patch_sends:
        copy.wait_send()
    early_sends[-1].wait_recv()
    for copy in passed:
        copy.wait()
    for copy in patch_sends:
        copy.wait_recv()

    def patch(step, carry):
        of = lax.rem(c + step, cols)
        base = pl.multiple_of(of * 64, 64)
        columns = patches[of, 0]
        for h, value in ((0, columns), (1, pltpu.roll(columns, 122, 1))):
            for start, mask in ((base, left_edge), (base + 7, right_edge)):
                at = pl.ds(start, 8, stride=8)
                band[h, at, :] = jnp.where(mask, value, band[h, at, :])
        for h, start, mask in (
            (0, base, at_lane < PASSES * TSIDE), (1, base + 56, at_lane >= 128 - PASSES * TSIDE)
        ):
            at = pl.ds(pl.multiple_of(start, 8), 8)
            band[h, at, :] = jnp.where(mask, patches[of, 1], band[h, at, :])
        return carry

    lax.fori_loop(1, cols, patch, 0, unroll=15)

    ones = jnp.ones((256, 128), jnp.bfloat16)
    group = 32

    def interact(g, carry):
        highs, lows = [], []
        for u in range(group):
            t = g * group + u
            for k in range(4):
                at = column[k, t] * 64 + tile[k, t]
                factor = right[t, k]
                high, low = split_bf16(
                    factor[:, :128] * band[0, pl.ds(at, 1), :] + factor[:, 128:] * band[1, pl.ds(at, 1), :]
                )
                highs.append(high)
                lows.append(low)
        parts = jnp.concatenate([jnp.concatenate(highs, axis=0), jnp.concatenate(lows, axis=0)], axis=1)
        coefficients = jnp.dot(parts, ones, preferred_element_type=F32)
        sums = [[], []]
        for u in range(group):
            t = g * group + u
            factor = left[t].reshape(64, 256)
            scale = coefficients[u * 64:(u + 1) * 64]
            for h in range(2):
                sums[h].append(jnp.sum(factor[:, h * 128:(h + 1) * 128] * scale, axis=0, keepdims=True))
        at = pl.ds(pl.multiple_of(g * group, group), group)
        for h in range(2):
            near[h, at, :] = near[h, at, :] + jnp.concatenate(sums[h], axis=0)
        return carry

    lax.fori_loop(0, 64 // group, interact, 0)

    laid = []
    for h in range(2):
        laid += swap_blocks([near[h, pl.ds(e, 8, stride=8), :] for e in range(8)])
    for i in range(TSIDE):
        pressure_out[pl.ds(i, 8, stride=TSIDE), :] = laid[i]


def local(
    opening_old, pressure_old, injection, front_flags, self_kernel,
    source_column, source_tile, source_rank, left_factor, right_factor,
):
    rows, cols = lax.axis_size("row"), lax.axis_size("col")
    anywhere = pl.BlockSpec(memory_space=pl.ANY)
    out = jax.ShapeDtypeStruct((128, 128), F32)
    lists = [a[0].T for a in (source_column, source_tile, source_rank)]
    operands = (opening_old, pressure_old, injection, front_flags, self_kernel, *lists, left_factor[0], right_factor[0])
    dma = pltpu.SemaphoreType.DMA
    return pl.pallas_call(
        functools.partial(kernel, rows, cols),
        out_shape=(out, out),
        in_specs=[anywhere] * 10,
        out_specs=(pl.BlockSpec(memory_space=pltpu.VMEM),) * 2,
        scratch_shapes=[
            pltpu.VMEM((3, 128, 128), F32),
            pltpu.VMEM((3, 128, 128), F32),
            pltpu.VMEM((3, 128, 128), F32),
            pltpu.VMEM((6, 3, 8, 128), F32),
            pltpu.VMEM((3, 128, 128), F32),
            pltpu.VMEM((128, 128), F32),
            pltpu.VMEM((2, 64, 128), F32),
            pltpu.VMEM((2, 64 * cols, 128), F32),
            pltpu.VMEM((cols, 2, 8, 128), F32),
            pltpu.VMEM((64, 4, 16, 256), F32),
            pltpu.VMEM((64, 4, 16, 256), F32),
            pltpu.VMEM((256, 256), F32),
            pltpu.VMEM((1, 64), jnp.int32),
            pltpu.VMEM((2, 64, 128), F32),
            pltpu.SMEM((4, 64), jnp.int32),
            pltpu.SMEM((4, 64), jnp.int32),
            pltpu.SMEM((4, 64), jnp.int32),
            dma((3,)),
            dma((5,)),
            dma((2,)),
            dma((8,)),
            dma((8,)),
            dma((8,)),
            dma((8,)),
            dma((8,)),
            dma((8,)),
            dma((16,)),
            dma((16,)),
        ],
        compiler_params=pltpu.CompilerParams(
            collective_id=0, has_side_effects=True, vmem_limit_bytes=40 * 1024 * 1024
        ),
        name="fracture",
    )(*[pltpu.with_memory_space_constraint(a, pltpu.HBM) for a in operands])


def solution(mesh):
    fields, lists, factors = P("row", "col"), P("row", "col", None), P("row", "col", None, None, None)
    return jax.shard_map(
        local,
        mesh=mesh,
        in_specs=(fields, fields, fields, fields, P(), lists, lists, lists, factors, factors),
        out_specs=(fields, fields),
        check_vma=False,
    )
```

```python
import functools

import jax
import jax.numpy as jnp
from jax import lax
from jax.experimental import pallas as pl
from jax.experimental.pallas import tpu as pltpu
from jax.sharding import PartitionSpec as P

TSIDE = 16
PASSES = 3
STEP = 0.1
MESH = pl.DeviceIdType.MESH
F32 = jnp.float32
HIGHEST = lax.Precision.HIGHEST


def swap_blocks(parts):
    parts = list(parts)
    block = lax.broadcasted_iota(jnp.int32, (8, 128), 1) // TSIDE
    for bit in (1, 2, 4):
        upper = (block & bit) != 0
        for i in range(8):
            if i & bit:
                continue
            a, b = parts[i], parts[i + bit]
            parts[i] = jnp.where(upper, pltpu.roll(b, TSIDE * bit, 1), a)
            parts[i + bit] = jnp.where(upper, b, pltpu.roll(a, 128 - TSIDE * bit, 1))
    return parts


def split_bf16(x):
    high = x.astype(jnp.bfloat16)
    low = (x - high.astype(F32)).astype(jnp.bfloat16)
    return high, low


def flat_tiles(rows_of):
    return swap_blocks(rows_of[:8]), swap_blocks(rows_of[8:])


def kernel(
    rows, cols,
    opening_ref, pressure_ref, injection_ref, flags_ref, self_ref,
    column_ref, tile_ref, rank_ref, left_ref, right_ref,
    results,
    field, turned, from_side, edge_rows, edge_cols, middle, early, band, patches, left, right, self_kernel, flags, near,
    column, tile, rank,
    field_sem, small_sem, factor_sem, edge_send, edge_recv, early_send, early_recv, pass_send, pass_recv,
    patch_send, patch_recv,
):
    r, c = lax.axis_index("row"), lax.axis_index("col")
    west, east = lax.rem(c + cols - 1, cols), lax.rem(c + 1, cols)
    has_north, has_south = r > 0, r < rows - 1
    north, south = jnp.maximum(r - 1, 0), jnp.minimum(r + 1, rows - 1)

    field_copies = [
        pltpu.make_async_copy(ref, field.at[i], field_sem.at[i])
        for i, ref in enumerate((opening_ref, pressure_ref, injection_ref))
    ]
    small_copies = [
        pltpu.make_async_copy(ref, to, small_sem.at[i])
        for i, (ref, to) in enumerate(
            ((flags_ref, flags), (self_ref, self_kernel), (column_ref, column), (tile_ref, tile), (rank_ref, rank))
        )
    ]
    factor_copies = [
        pltpu.make_async_copy(right_ref, right, factor_sem.at[0]),
        pltpu.make_async_copy(left_ref, left, factor_sem.at[1]),
    ]
    for copy in field_copies + small_copies:
        copy.start()

    barrier = pltpu.get_barrier_semaphore()
    for there, to in ((has_north, north), (has_south, south)):
        @pl.when(there)
        def _():
            for beside in (c, west, east):
                pl.semaphore_signal(barrier, inc=1, device_id=(to, beside), device_id_type=MESH)
    for step in range(1, cols):
        pl.semaphore_signal(
            barrier, inc=1, device_id=(r, lax.rem(c + step, cols)), device_id_type=MESH
        )

    for copy in field_copies:
        copy.wait()
    for i in range(3):
        turned[i] = field[i].T
    edge_cols[:, pl.ds(8, 112), :] = jnp.zeros((3, 112, 128), F32)

    sends, sends_north, sends_south = [], [], []
    top, bottom = pl.ds(0, 8), pl.ds(120, 8)

    def edge(src, dst, slot, target, to):
        to.append(pltpu.make_async_remote_copy(
            src_ref=src, dst_ref=dst, send_sem=edge_send.at[slot], recv_sem=edge_recv.at[slot],
            device_id=target, device_id_type=MESH,
        ))

    edge(field.at[:, top, :], edge_rows.at[5], 5, (north, west), sends_north)
    edge(field.at[:, top, :], edge_rows.at[4], 4, (north, east), sends_north)
    edge(field.at[:, top, :], edge_rows.at[1], 1, (north, c), sends_north)
    edge(field.at[:, bottom, :], edge_rows.at[3], 3, (south, west), sends_south)
    edge(field.at[:, bottom, :], edge_rows.at[2], 2, (south, east), sends_south)
    edge(field.at[:, bottom, :], edge_rows.at[0], 0, (south, c), sends_south)
    edge(turned.at[:, top, :], edge_cols.at[:, top, :], 6, (r, west), sends)
    edge(turned.at[:, bottom, :], edge_cols.at[:, bottom, :], 7, (r, east), sends)

    pl.semaphore_wait(
        barrier, 3 * has_north.astype(jnp.int32) + 3 * has_south.astype(jnp.int32) + cols - 1
    )

    for there, group in ((has_north, sends_north), (has_south, sends_south)):
        @pl.when(there)
        def _():
            for copy in group:
                copy.start()
    for copy in sends:
        copy.start()

    small_copies[0].wait()
    lane = lax.broadcasted_iota(jnp.int32, (8, 64), 1)
    sub = lax.broadcasted_iota(jnp.int32, (8, 64), 0)
    spread = jnp.where(lane // 8 == sub, flags[...].astype(F32), 0.0)
    from_tile = lax.broadcasted_iota(jnp.int32, (64, 128), 0)
    to_lane = lax.broadcasted_iota(jnp.int32, (64, 128), 1)
    inside = jnp.dot(
        spread, (from_tile % 8 == to_lane // TSIDE).astype(F32), preferred_element_type=F32
    )

    def passes(start, press, source, keep):
        height, width = start.shape
        across = (pltpu.roll(press, width - 1, 1) - press) / 24.0
        down = (pltpu.roll(press, height - 1, 0) - press) / 24.0
        current = start
        for _ in range(PASSES):
            cubed = current * current * current
            flux_across = (cubed + pltpu.roll(cubed, width - 1, 1)) * across
            flux_down = (cubed + pltpu.roll(cubed, height - 1, 0)) * down
            total = (flux_across - pltpu.roll(flux_across, 1, 1)) + (flux_down - pltpu.roll(flux_down, 1, 0))
            current = keep(start + STEP * (total + source))
        return current

    middle[...] = passes(field[0], field[1], field[2], lambda v: v)
    first, second = flat_tiles([middle[pl.ds(i, 8, stride=TSIDE), :] * inside for i in range(TSIDE)])
    for e in range(8):
        early[0, pl.ds(e, 8, stride=8), :] = first[e]
        early[1, pl.ds(e, 8, stride=8), :] = second[e]

    def block(of):
        return band.at[:, pl.ds(pl.multiple_of(of * 64, 64), 64), :]

    sibling = (r, c ^ 1)
    chips = (4, 5, 3, 7, 1, 2, 6)
    early_sends = [
        pltpu.make_async_remote_copy(
            src_ref=early, dst_ref=block(c), send_sem=early_send.at[i], recv_sem=early_recv.at[i],
            device_id=sibling if i == 0 else (r, c ^ (2 * i)), device_id_type=MESH,
        )
        for i in chips + (0,)
    ]
    for copy in early_sends + factor_copies:
        copy.start()

    wide_rows, wide_cols = 136, 256
    at_row = lax.broadcasted_iota(jnp.int32, (wide_rows, wide_cols), 0)
    at_col = lax.broadcasted_iota(jnp.int32, (wide_rows, wide_cols), 1)
    low_row = jnp.where(r == rows - 1, 128, 132)
    high_row = jnp.where(r == 0, 136, 132)
    low_col = jnp.where(c == cols - 1, 128, 192)
    high_col = jnp.where(c == 0, 256, 192)
    valid = ((at_row < low_row) | (at_row >= high_row)) & ((at_col < low_col) | (at_col >= high_col))
    upper_half = lax.broadcasted_iota(jnp.int32, (8, 128), 0) < 4
    left_half = lax.broadcasted_iota(jnp.int32, (8, 128), 1) < 64

    for copy in sends:
        copy.wait_recv()
    for i in range(3):
        from_side[i] = edge_cols[i].T
    for there, group in ((has_south, sends_north), (has_north, sends_south)):
        @pl.when(there)
        def _():
            for copy in group:
                copy.wait_recv()
    wide = []
    for i in range(3):
        under = jnp.where(upper_half, edge_rows[1, i], edge_rows[0, i])
        corner = jnp.where(
            left_half,
            jnp.where(upper_half, edge_rows[5, i], edge_rows[3, i]),
            jnp.where(upper_half, edge_rows[4, i], edge_rows[2, i]),
        )
        whole = jnp.concatenate(
            [jnp.concatenate([field[i], from_side[i]], axis=1), jnp.concatenate([under, corner], axis=1)], axis=0
        )
        wide.append(jnp.where(valid, whole, 0.0))
    current = passes(*wide, lambda v: jnp.where(valid, v, 0.0))
    middle[...] = current[:128, :128]

    own = pl.multiple_of(c * 64, 64)
    rows_of = [middle[pl.ds(i, 8, stride=TSIDE), :] * inside for i in range(TSIDE)]
    first, second = flat_tiles(rows_of)
    for e in range(8):
        band[0, pl.ds(own + e, 8, stride=8), :] = first[e]
        band[1, pl.ds(own + e, 8, stride=8), :] = second[e]

    at_lane = lax.broadcasted_iota(jnp.int32, (8, 128), 1)
    in_row = at_lane % TSIDE
    left_edge, right_edge = in_row < PASSES, in_row >= TSIDE - PASSES
    outer = left_edge | right_edge
    ends = [jnp.where(in_row < TSIDE // 2, half[0], half[7]) for half in (first, second)]
    patches[c, 0] = jnp.where(outer, ends[0], pltpu.roll(ends[1], 6, 1))
    patches[c, 1] = jnp.where(
        left_half, band[0, pl.ds(own, 8), :], band[1, pl.ds(pl.multiple_of(own + 56, 8), 8), :]
    )
    patch_sends = []
    for step in (10, 11, 6, 7, 14, 15, 8, 9, 4, 5, 12, 13, 2, 3, 1):
        copy = pltpu.make_async_remote_copy(
            src_ref=patches.at[c], dst_ref=patches.at[c],
            send_sem=patch_send.at[step], recv_sem=patch_recv.at[step],
            device_id=(r, c ^ step), device_id_type=MESH,
        )
        copy.start()
        patch_sends.append(copy)
    for i in range(TSIDE):
        results[0, pl.ds(i, 8, stride=TSIDE), :] = rows_of[i]

    passed = []
    for n, i in enumerate(chips):
        early_sends[n].wait_recv()
        copy = pltpu.make_async_remote_copy(
            src_ref=block(c ^ (2 * i)), dst_ref=block(c ^ (2 * i)),
            send_sem=pass_send.at[i], recv_sem=pass_recv.at[i],
            device_id=sibling, device_id_type=MESH,
        )
        copy.start()
        passed.append(copy)

    small_copies[1].wait()
    own_tiles = jnp.concatenate([band[h, pl.ds(own, 64), :] for h in range(2)], axis=1)
    own_term = lax.dot_general(
        own_tiles, self_kernel[...], (((1,), (1,)), ((), ())), precision=HIGHEST, preferred_element_type=F32
    )
    near[0], near[1] = own_term[:, :128], own_term[:, 128:]
    for copy in small_copies[2:]:
        copy.wait()
    for copy in factor_copies:
        copy.wait()

    at_rank = lax.broadcasted_iota(jnp.int32, (16, 256), 0)

    def cut(t, carry):
        for k in range(4):
            left[t, k] = jnp.where(at_rank < rank[k, t], left[t, k], 0.0)
        return carry

    lax.fori_loop(0, 64, cut, 0)
    for there, group in ((has_north, sends_north), (has_south, sends_south)):
        @pl.when(there)
        def _():
            for copy in group:
                copy.wait_send()
    for copy in sends + early_sends + patch_sends:
        copy.wait_send()
    early_sends[-1].wait_recv()
    for copy in passed:
        copy.wait()
    for copy in patch_sends:
        copy.wait_recv()

    def patch(step, carry):
        of = lax.rem(c + step, cols)
        base = pl.multiple_of(of * 64, 64)
        columns = patches[of, 0]
        for h, value in ((0, columns), (1, pltpu.roll(columns, 122, 1))):
            for start, mask in ((base, left_edge), (base + 7, right_edge)):
                at = pl.ds(start, 8, stride=8)
                band[h, at, :] = jnp.where(mask, value, band[h, at, :])
        for h, start, mask in (
            (0, base, at_lane < PASSES * TSIDE), (1, base + 56, at_lane >= 128 - PASSES * TSIDE)
        ):
            at = pl.ds(pl.multiple_of(start, 8), 8)
            band[h, at, :] = jnp.where(mask, patches[of, 1], band[h, at, :])
        return carry

    lax.fori_loop(1, cols, patch, 0, unroll=15)

    ones = jnp.ones((256, 128), jnp.bfloat16)
    group = 32

    def interact(g, carry):
        highs, lows = [], []
        for u in range(group):
            t = g * group + u
            for k in range(4):
                at = column[k, t] * 64 + tile[k, t]
                factor = right[t, k]
                high, low = split_bf16(
                    factor[:, :128] * band[0, pl.ds(at, 1), :] + factor[:, 128:] * band[1, pl.ds(at, 1), :]
                )
                highs.append(high)
                lows.append(low)
        parts = jnp.concatenate([jnp.concatenate(highs, axis=0), jnp.concatenate(lows, axis=0)], axis=1)
        coefficients = jnp.dot(parts, ones, preferred_element_type=F32)
        sums = [[], []]
        for u in range(group):
            t = g * group + u
            factor = left[t].reshape(64, 256)
            scale = coefficients[u * 64:(u + 1) * 64]
            for h in range(2):
                sums[h].append(jnp.sum(factor[:, h * 128:(h + 1) * 128] * scale, axis=0, keepdims=True))
        at = pl.ds(pl.multiple_of(g * group, group), group)
        for h in range(2):
            near[h, at, :] = near[h, at, :] + jnp.concatenate(sums[h], axis=0)
        return carry

    lax.fori_loop(0, 64 // group, interact, 0)

    laid = []
    for h in range(2):
        laid += swap_blocks([near[h, pl.ds(e, 8, stride=8), :] for e in range(8)])
    for i in range(TSIDE):
        results[1, pl.ds(i, 8, stride=TSIDE), :] = laid[i]


def local(
    opening_old, pressure_old, injection, front_flags, self_kernel,
    source_column, source_tile, source_rank, left_factor, right_factor,
):
    rows, cols = lax.axis_size("row"), lax.axis_size("col")
    anywhere = pl.BlockSpec(memory_space=pl.ANY)
    out = jax.ShapeDtypeStruct((2, 128, 128), F32)
    lists = [a[0].T for a in (source_column, source_tile, source_rank)]
    operands = (opening_old, pressure_old, injection, front_flags, self_kernel, *lists, left_factor[0], right_factor[0])
    dma = pltpu.SemaphoreType.DMA
    both = pl.pallas_call(
        functools.partial(kernel, rows, cols),
        out_shape=out,
        in_specs=[anywhere] * 10,
        out_specs=pl.BlockSpec(memory_space=pltpu.VMEM),
        scratch_shapes=[
            pltpu.VMEM((3, 128, 128), F32),
            pltpu.VMEM((3, 128, 128), F32),
            pltpu.VMEM((3, 128, 128), F32),
            pltpu.VMEM((6, 3, 8, 128), F32),
            pltpu.VMEM((3, 128, 128), F32),
            pltpu.VMEM((128, 128), F32),
            pltpu.VMEM((2, 64, 128), F32),
            pltpu.VMEM((2, 64 * cols, 128), F32),
            pltpu.VMEM((cols, 2, 8, 128), F32),
            pltpu.VMEM((64, 4, 16, 256), F32),
            pltpu.VMEM((64, 4, 16, 256), F32),
            pltpu.VMEM((256, 256), F32),
            pltpu.VMEM((1, 64), jnp.int32),
            pltpu.VMEM((2, 64, 128), F32),
            pltpu.SMEM((4, 64), jnp.int32),
            pltpu.SMEM((4, 64), jnp.int32),
            pltpu.SMEM((4, 64), jnp.int32),
            dma((3,)),
            dma((5,)),
            dma((2,)),
            dma((8,)),
            dma((8,)),
            dma((8,)),
            dma((8,)),
            dma((8,)),
            dma((8,)),
            dma((16,)),
            dma((16,)),
        ],
        compiler_params=pltpu.CompilerParams(
            collective_id=0, has_side_effects=True, vmem_limit_bytes=40 * 1024 * 1024
        ),
        name="fracture",
    )(*[pltpu.with_memory_space_constraint(a, pltpu.HBM) for a in operands])
    return both[0], both[1]


def solution(mesh):
    fields, lists, factors = P("row", "col"), P("row", "col", None), P("row", "col", None, None, None)
    return jax.shard_map(
        local,
        mesh=mesh,
        in_specs=(fields, fields, fields, fields, P(), lists, lists, lists, factors, factors),
        out_specs=(fields, fields),
        check_vma=False,
    )
```

```python
import functools

import jax
import jax.numpy as jnp
from jax import lax
from jax.experimental import pallas as pl
from jax.experimental.pallas import tpu as pltpu
from jax.sharding import PartitionSpec as P

TSIDE = 16
PASSES = 3
STEP = 0.1
MESH = pl.DeviceIdType.MESH
F32 = jnp.float32
HIGHEST = lax.Precision.HIGHEST


def swap_blocks(parts):
    parts = list(parts)
    block = lax.broadcasted_iota(jnp.int32, (8, 128), 1) // TSIDE
    for bit in (1, 2, 4):
        upper = (block & bit) != 0
        for i in range(8):
            if i & bit:
                continue
            a, b = parts[i], parts[i + bit]
            parts[i] = jnp.where(upper, pltpu.roll(b, TSIDE * bit, 1), a)
            parts[i + bit] = jnp.where(upper, b, pltpu.roll(a, 128 - TSIDE * bit, 1))
    return parts


def split_bf16(x):
    high = x.astype(jnp.bfloat16)
    low = (x - high.astype(F32)).astype(jnp.bfloat16)
    return high, low


def flat_tiles(rows_of):
    return swap_blocks(rows_of[:8]), swap_blocks(rows_of[8:])


def kernel(
    rows, cols,
    opening_ref, pressure_ref, injection_ref, flags_ref, self_ref,
    column_ref, tile_ref, rank_ref, left_ref, right_ref,
    results,
    field, turned, from_side, edge_rows, edge_cols, middle, early, band, patches, left, right, self_kernel, flags, near,
    column, tile, rank,
    field_sem, small_sem, factor_sem, edge_send, edge_recv, early_send, early_recv, pass_send, pass_recv,
    patch_send, patch_recv,
):
    r, c = lax.axis_index("row"), lax.axis_index("col")
    west, east = lax.rem(c + cols - 1, cols), lax.rem(c + 1, cols)
    has_north, has_south = r > 0, r < rows - 1
    north, south = jnp.maximum(r - 1, 0), jnp.minimum(r + 1, rows - 1)

    field_copies = [
        pltpu.make_async_copy(ref, field.at[i], field_sem.at[i])
        for i, ref in enumerate((opening_ref, pressure_ref, injection_ref))
    ]
    small_copies = [
        pltpu.make_async_copy(ref, to, small_sem.at[i])
        for i, (ref, to) in enumerate(
            ((flags_ref, flags), (self_ref, self_kernel), (column_ref, column), (tile_ref, tile), (rank_ref, rank))
        )
    ]
    factor_copies = [
        pltpu.make_async_copy(right_ref, right, factor_sem.at[0]),
        pltpu.make_async_copy(left_ref, left, factor_sem.at[1]),
    ]
    for copy in field_copies + small_copies:
        copy.start()

    barrier = pltpu.get_barrier_semaphore()
    for there, to in ((has_north, north), (has_south, south)):
        @pl.when(there)
        def _():
            for beside in (c, west, east):
                pl.semaphore_signal(barrier, inc=1, device_id=(to, beside), device_id_type=MESH)
    for step in range(1, cols):
        pl.semaphore_signal(
            barrier, inc=1, device_id=(r, lax.rem(c + step, cols)), device_id_type=MESH
        )

    for copy in field_copies:
        copy.wait()
    for i in range(3):
        turned[i] = field[i].T
    edge_cols[:, pl.ds(8, 112), :] = jnp.zeros((3, 112, 128), F32)

    sends, sends_north, sends_south = [], [], []
    top, bottom = pl.ds(0, 8), pl.ds(120, 8)

    def edge(src, dst, slot, target, to):
        to.append(pltpu.make_async_remote_copy(
            src_ref=src, dst_ref=dst, send_sem=edge_send.at[slot], recv_sem=edge_recv.at[slot],
            device_id=target, device_id_type=MESH,
        ))

    edge(field.at[:, top, :], edge_rows.at[5], 5, (north, west), sends_north)
    edge(field.at[:, top, :], edge_rows.at[4], 4, (north, east), sends_north)
    edge(field.at[:, top, :], edge_rows.at[1], 1, (north, c), sends_north)
    edge(field.at[:, bottom, :], edge_rows.at[3], 3, (south, west), sends_south)
    edge(field.at[:, bottom, :], edge_rows.at[2], 2, (south, east), sends_south)
    edge(field.at[:, bottom, :], edge_rows.at[0], 0, (south, c), sends_south)
    edge(turned.at[:, top, :], edge_cols.at[:, top, :], 6, (r, west), sends)
    edge(turned.at[:, bottom, :], edge_cols.at[:, bottom, :], 7, (r, east), sends)

    small_copies[0].wait()
    lane = lax.broadcasted_iota(jnp.int32, (8, 64), 1)
    sub = lax.broadcasted_iota(jnp.int32, (8, 64), 0)
    spread = jnp.where(lane // 8 == sub, flags[...].astype(F32), 0.0)
    from_tile = lax.broadcasted_iota(jnp.int32, (64, 128), 0)
    to_lane = lax.broadcasted_iota(jnp.int32, (64, 128), 1)
    inside = jnp.dot(
        spread, (from_tile % 8 == to_lane // TSIDE).astype(F32), preferred_element_type=F32
    )

    def passes(start, press, source, keep):
        height, width = start.shape
        across = (pltpu.roll(press, width - 1, 1) - press) / 24.0
        down = (pltpu.roll(press, height - 1, 0) - press) / 24.0
        current = start
        for _ in range(PASSES):
            cubed = current * current * current
            flux_across = (cubed + pltpu.roll(cubed, width - 1, 1)) * across
            flux_down = (cubed + pltpu.roll(cubed, height - 1, 0)) * down
            total = (flux_across - pltpu.roll(flux_across, 1, 1)) + (flux_down - pltpu.roll(flux_down, 1, 0))
            current = keep(start + STEP * (total + source))
        return current

    middle[...] = passes(field[0], field[1], field[2], lambda v: v)
    first, second = flat_tiles([middle[pl.ds(i, 8, stride=TSIDE), :] * inside for i in range(TSIDE)])
    for e in range(8):
        early[0, pl.ds(e, 8, stride=8), :] = first[e]
        early[1, pl.ds(e, 8, stride=8), :] = second[e]

    def block(of):
        return band.at[:, pl.ds(pl.multiple_of(of * 64, 64), 64), :]

    sibling = (r, c ^ 1)
    chips = (4, 5, 3, 7, 1, 2, 6)
    early_sends = [
        pltpu.make_async_remote_copy(
            src_ref=early, dst_ref=block(c), send_sem=early_send.at[i], recv_sem=early_recv.at[i],
            device_id=sibling if i == 0 else (r, c ^ (2 * i)), device_id_type=MESH,
        )
        for i in chips + (0,)
    ]
    pl.semaphore_wait(
        barrier, 3 * has_north.astype(jnp.int32) + 3 * has_south.astype(jnp.int32) + cols - 1
    )

    for there, group in ((has_north, sends_north), (has_south, sends_south)):
        @pl.when(there)
        def _():
            for copy in group:
                copy.start()
    for copy in sends:
        copy.start()

    for core, order in ((0, (4, 5, 3, 7, 1, 2, 6, 0)), (1, (5, 3, 4, 7, 2, 1, 6, 0))):
        @pl.when(lax.rem(c, 2) == core)
        def _():
            for i in order:
                early_sends[chips.index(i) if i else 7].start()
    for copy in factor_copies:
        copy.start()

    wide_rows, wide_cols = 136, 256
    at_row = lax.broadcasted_iota(jnp.int32, (wide_rows, wide_cols), 0)
    at_col = lax.broadcasted_iota(jnp.int32, (wide_rows, wide_cols), 1)
    low_row = jnp.where(r == rows - 1, 128, 132)
    high_row = jnp.where(r == 0, 136, 132)
    low_col = jnp.where(c == cols - 1, 128, 192)
    high_col = jnp.where(c == 0, 256, 192)
    valid = ((at_row < low_row) | (at_row >= high_row)) & ((at_col < low_col) | (at_col >= high_col))
    upper_half = lax.broadcasted_iota(jnp.int32, (8, 128), 0) < 4
    left_half = lax.broadcasted_iota(jnp.int32, (8, 128), 1) < 64

    for copy in sends:
        copy.wait_recv()
    for i in range(3):
        from_side[i] = edge_cols[i].T
    for there, group in ((has_south, sends_north), (has_north, sends_south)):
        @pl.when(there)
        def _():
            for copy in group:
                copy.wait_recv()
    wide = []
    for i in range(3):
        under = jnp.where(upper_half, edge_rows[1, i], edge_rows[0, i])
        corner = jnp.where(
            left_half,
            jnp.where(upper_half, edge_rows[5, i], edge_rows[3, i]),
            jnp.where(upper_half, edge_rows[4, i], edge_rows[2, i]),
        )
        whole = jnp.concatenate(
            [jnp.concatenate([field[i], from_side[i]], axis=1), jnp.concatenate([under, corner], axis=1)], axis=0
        )
        wide.append(jnp.where(valid, whole, 0.0))
    current = passes(*wide, lambda v: jnp.where(valid, v, 0.0))
    middle[...] = current[:128, :128]

    own = pl.multiple_of(c * 64, 64)
    rows_of = [middle[pl.ds(i, 8, stride=TSIDE), :] * inside for i in range(TSIDE)]
    first, second = flat_tiles(rows_of)
    for e in range(8):
        band[0, pl.ds(own + e, 8, stride=8), :] = first[e]
        band[1, pl.ds(own + e, 8, stride=8), :] = second[e]

    at_lane = lax.broadcasted_iota(jnp.int32, (8, 128), 1)
    in_row = at_lane % TSIDE
    left_edge, right_edge = in_row < PASSES, in_row >= TSIDE - PASSES
    outer = left_edge | right_edge
    ends = [jnp.where(in_row < TSIDE // 2, half[0], half[7]) for half in (first, second)]
    patches[c, 0] = jnp.where(outer, ends[0], pltpu.roll(ends[1], 6, 1))
    patches[c, 1] = jnp.where(
        left_half, band[0, pl.ds(own, 8), :], band[1, pl.ds(pl.multiple_of(own + 56, 8), 8), :]
    )
    patch_sends = []
    for step in (10, 11, 6, 7, 14, 15, 8, 9, 4, 5, 12, 13, 2, 3, 1):
        copy = pltpu.make_async_remote_copy(
            src_ref=patches.at[c], dst_ref=patches.at[c],
            send_sem=patch_send.at[step], recv_sem=patch_recv.at[step],
            device_id=(r, c ^ step), device_id_type=MESH,
        )
        copy.start()
        patch_sends.append(copy)
    for i in range(TSIDE):
        results[0, pl.ds(i, 8, stride=TSIDE), :] = rows_of[i]

    passed = []
    for n, i in enumerate(chips):
        early_sends[n].wait_recv()
        copy = pltpu.make_async_remote_copy(
            src_ref=block(c ^ (2 * i)), dst_ref=block(c ^ (2 * i)),
            send_sem=pass_send.at[i], recv_sem=pass_recv.at[i],
            device_id=sibling, device_id_type=MESH,
        )
        copy.start()
        passed.append(copy)

    small_copies[1].wait()
    own_tiles = jnp.concatenate([band[h, pl.ds(own, 64), :] for h in range(2)], axis=1)
    own_term = lax.dot_general(
        own_tiles, self_kernel[...], (((1,), (1,)), ((), ())), precision=HIGHEST, preferred_element_type=F32
    )
    near[0], near[1] = own_term[:, :128], own_term[:, 128:]
    for copy in small_copies[2:]:
        copy.wait()
    for copy in factor_copies:
        copy.wait()

    at_rank = lax.broadcasted_iota(jnp.int32, (16, 256), 0)

    def cut(t, carry):
        for k in range(4):
            left[t, k] = jnp.where(at_rank < rank[k, t], left[t, k], 0.0)
        return carry

    lax.fori_loop(0, 64, cut, 0)
    for there, group in ((has_north, sends_north), (has_south, sends_south)):
        @pl.when(there)
        def _():
            for copy in group:
                copy.wait_send()
    for copy in sends + early_sends + patch_sends:
        copy.wait_send()
    early_sends[-1].wait_recv()
    for copy in passed:
        copy.wait()
    for copy in patch_sends:
        copy.wait_recv()

    def patch(step, carry):
        of = lax.rem(c + step, cols)
        base = pl.multiple_of(of * 64, 64)
        columns = patches[of, 0]
        for h, value in ((0, columns), (1, pltpu.roll(columns, 122, 1))):
            for start, mask in ((base, left_edge), (base + 7, right_edge)):
                at = pl.ds(start, 8, stride=8)
                band[h, at, :] = jnp.where(mask, value, band[h, at, :])
        for h, start, mask in (
            (0, base, at_lane < PASSES * TSIDE), (1, base + 56, at_lane >= 128 - PASSES * TSIDE)
        ):
            at = pl.ds(pl.multiple_of(start, 8), 8)
            band[h, at, :] = jnp.where(mask, patches[of, 1], band[h, at, :])
        return carry

    lax.fori_loop(1, cols, patch, 0, unroll=15)

    ones = jnp.ones((256, 128), jnp.bfloat16)
    group = 64

    def interact(g, carry):
        highs, lows = [], []
        for u in range(group):
            t = g * group + u
            for k in range(4):
                at = column[k, t] * 64 + tile[k, t]
                factor = right[t, k]
                high, low = split_bf16(
                    factor[:, :128] * band[0, pl.ds(at, 1), :] + factor[:, 128:] * band[1, pl.ds(at, 1), :]
                )
                highs.append(high)
                lows.append(low)
        parts = jnp.concatenate([jnp.concatenate(highs, axis=0), jnp.concatenate(lows, axis=0)], axis=1)
        coefficients = jnp.dot(parts, ones, preferred_element_type=F32)
        sums = [[], []]
        for u in range(group):
            t = g * group + u
            factor = left[t].reshape(64, 256)
            scale = coefficients[u * 64:(u + 1) * 64]
            for h in range(2):
                sums[h].append(jnp.sum(factor[:, h * 128:(h + 1) * 128] * scale, axis=0, keepdims=True))
        at = pl.ds(pl.multiple_of(g * group, group), group)
        for h in range(2):
            near[h, at, :] = near[h, at, :] + jnp.concatenate(sums[h], axis=0)
        return carry

    lax.fori_loop(0, 64 // group, interact, 0)

    laid = []
    for h in range(2):
        laid += swap_blocks([near[h, pl.ds(e, 8, stride=8), :] for e in range(8)])
    for i in range(TSIDE):
        results[1, pl.ds(i, 8, stride=TSIDE), :] = laid[i]


def local(
    opening_old, pressure_old, injection, front_flags, self_kernel,
    source_column, source_tile, source_rank, left_factor, right_factor,
):
    rows, cols = lax.axis_size("row"), lax.axis_size("col")
    anywhere = pl.BlockSpec(memory_space=pl.ANY)
    out = jax.ShapeDtypeStruct((2, 128, 128), F32)
    lists = [a[0].T for a in (source_column, source_tile, source_rank)]
    operands = (opening_old, pressure_old, injection, front_flags, self_kernel, *lists, left_factor[0], right_factor[0])
    dma = pltpu.SemaphoreType.DMA
    both = pl.pallas_call(
        functools.partial(kernel, rows, cols),
        out_shape=out,
        in_specs=[anywhere] * 10,
        out_specs=pl.BlockSpec(memory_space=pltpu.VMEM),
        scratch_shapes=[
            pltpu.VMEM((3, 128, 128), F32),
            pltpu.VMEM((3, 128, 128), F32),
            pltpu.VMEM((3, 128, 128), F32),
            pltpu.VMEM((6, 3, 8, 128), F32),
            pltpu.VMEM((3, 128, 128), F32),
            pltpu.VMEM((128, 128), F32),
            pltpu.VMEM((2, 64, 128), F32),
            pltpu.VMEM((2, 64 * cols, 128), F32),
            pltpu.VMEM((cols, 2, 8, 128), F32),
            pltpu.VMEM((64, 4, 16, 256), F32),
            pltpu.VMEM((64, 4, 16, 256), F32),
            pltpu.VMEM((256, 256), F32),
            pltpu.VMEM((1, 64), jnp.int32),
            pltpu.VMEM((2, 64, 128), F32),
            pltpu.SMEM((4, 64), jnp.int32),
            pltpu.SMEM((4, 64), jnp.int32),
            pltpu.SMEM((4, 64), jnp.int32),
            dma((3,)),
            dma((5,)),
            dma((2,)),
            dma((8,)),
            dma((8,)),
            dma((8,)),
            dma((8,)),
            dma((8,)),
            dma((8,)),
            dma((16,)),
            dma((16,)),
        ],
        compiler_params=pltpu.CompilerParams(
            collective_id=0, has_side_effects=True, vmem_limit_bytes=40 * 1024 * 1024
        ),
        name="fracture",
    )(*[pltpu.with_memory_space_constraint(a, pltpu.HBM) for a in operands])
    return both[0], both[1]


def solution(mesh):
    fields, lists, factors = P("row", "col"), P("row", "col", None), P("row", "col", None, None, None)
    return jax.shard_map(
        local,
        mesh=mesh,
        in_specs=(fields, fields, fields, fields, P(), lists, lists, lists, factors, factors),
        out_specs=(fields, fields),
        check_vma=False,
    )
```

```python
import functools

import jax
import jax.numpy as jnp
from jax import lax
from jax.experimental import pallas as pl
from jax.experimental.pallas import tpu as pltpu
from jax.sharding import PartitionSpec as P

TSIDE = 16
PASSES = 3
STEP = 0.1
MESH = pl.DeviceIdType.MESH
F32 = jnp.float32
HIGHEST = lax.Precision.HIGHEST


def swap_blocks(parts):
    parts = list(parts)
    block = lax.broadcasted_iota(jnp.int32, (8, 128), 1) // TSIDE
    for bit in (1, 2, 4):
        upper = (block & bit) != 0
        for i in range(8):
            if i & bit:
                continue
            a, b = parts[i], parts[i + bit]
            parts[i] = jnp.where(upper, pltpu.roll(b, TSIDE * bit, 1), a)
            parts[i + bit] = jnp.where(upper, b, pltpu.roll(a, 128 - TSIDE * bit, 1))
    return parts


def split_bf16(x):
    high = x.astype(jnp.bfloat16)
    low = (x - high.astype(F32)).astype(jnp.bfloat16)
    return high, low


def flat_tiles(rows_of):
    return swap_blocks(rows_of[:8]), swap_blocks(rows_of[8:])


def kernel(
    rows, cols,
    opening_ref, pressure_ref, injection_ref, flags_ref, self_ref,
    column_ref, tile_ref, rank_ref, left_ref, right_ref,
    results,
    field, turned, from_side, edge_rows, edge_cols, middle, early, band, patches, left, right, self_kernel, flags, near,
    column, tile, rank,
    field_sem, small_sem, factor_sem, edge_send, edge_recv, early_send, early_recv, pass_send, pass_recv,
    patch_send, patch_recv,
):
    r, c = lax.axis_index("row"), lax.axis_index("col")
    west, east = lax.rem(c + cols - 1, cols), lax.rem(c + 1, cols)
    has_north, has_south = r > 0, r < rows - 1
    north, south = jnp.maximum(r - 1, 0), jnp.minimum(r + 1, rows - 1)

    field_copies = [
        pltpu.make_async_copy(ref, field.at[i], field_sem.at[i])
        for i, ref in enumerate((opening_ref, pressure_ref, injection_ref))
    ]
    small_copies = [
        pltpu.make_async_copy(ref, to, small_sem.at[i])
        for i, (ref, to) in enumerate(
            ((flags_ref, flags), (self_ref, self_kernel), (column_ref, column), (tile_ref, tile), (rank_ref, rank))
        )
    ]
    factor_copies = [
        pltpu.make_async_copy(right_ref, right, factor_sem.at[0]),
        pltpu.make_async_copy(left_ref, left, factor_sem.at[1]),
    ]
    for copy in field_copies + small_copies:
        copy.start()

    barrier = pltpu.get_barrier_semaphore()
    for there, to in ((has_north, north), (has_south, south)):
        @pl.when(there)
        def _():
            for beside in (c, west, east):
                pl.semaphore_signal(barrier, inc=1, device_id=(to, beside), device_id_type=MESH)
    for step in range(1, cols):
        pl.semaphore_signal(
            barrier, inc=1, device_id=(r, lax.rem(c + step, cols)), device_id_type=MESH
        )

    for copy in field_copies:
        copy.wait()
    for i in range(3):
        turned[i] = field[i].T
    edge_cols[:, pl.ds(8, 112), :] = jnp.zeros((3, 112, 128), F32)

    sends, sends_north, sends_south = [], [], []
    top, bottom = pl.ds(0, 8), pl.ds(120, 8)

    def edge(src, dst, slot, target, to):
        to.append(pltpu.make_async_remote_copy(
            src_ref=src, dst_ref=dst, send_sem=edge_send.at[slot], recv_sem=edge_recv.at[slot],
            device_id=target, device_id_type=MESH,
        ))

    edge(field.at[:, top, :], edge_rows.at[5], 5, (north, west), sends_north)
    edge(field.at[:, top, :], edge_rows.at[4], 4, (north, east), sends_north)
    edge(field.at[:, top, :], edge_rows.at[1], 1, (north, c), sends_north)
    edge(field.at[:, bottom, :], edge_rows.at[3], 3, (south, west), sends_south)
    edge(field.at[:, bottom, :], edge_rows.at[2], 2, (south, east), sends_south)
    edge(field.at[:, bottom, :], edge_rows.at[0], 0, (south, c), sends_south)
    edge(turned.at[:, top, :], edge_cols.at[:, top, :], 6, (r, west), sends)
    edge(turned.at[:, bottom, :], edge_cols.at[:, bottom, :], 7, (r, east), sends)

    small_copies[0].wait()
    lane = lax.broadcasted_iota(jnp.int32, (8, 64), 1)
    sub = lax.broadcasted_iota(jnp.int32, (8, 64), 0)
    spread = jnp.where(lane // 8 == sub, flags[...].astype(F32), 0.0)
    from_tile = lax.broadcasted_iota(jnp.int32, (64, 128), 0)
    to_lane = lax.broadcasted_iota(jnp.int32, (64, 128), 1)
    inside = jnp.dot(
        spread, (from_tile % 8 == to_lane // TSIDE).astype(F32), preferred_element_type=F32
    )

    def passes(start, press, source, keep):
        height, width = start.shape
        across = (pltpu.roll(press, width - 1, 1) - press) / 24.0
        down = (pltpu.roll(press, height - 1, 0) - press) / 24.0
        current = start
        for _ in range(PASSES):
            cubed = current * current * current
            flux_across = (cubed + pltpu.roll(cubed, width - 1, 1)) * across
            flux_down = (cubed + pltpu.roll(cubed, height - 1, 0)) * down
            total = (flux_across - pltpu.roll(flux_across, 1, 1)) + (flux_down - pltpu.roll(flux_down, 1, 0))
            current = keep(start + STEP * (total + source))
        return current

    middle[...] = passes(field[0], field[1], field[2], lambda v: v)
    first, second = flat_tiles([middle[pl.ds(i, 8, stride=TSIDE), :] * inside for i in range(TSIDE)])
    for e in range(8):
        early[0, pl.ds(e, 8, stride=8), :] = first[e]
        early[1, pl.ds(e, 8, stride=8), :] = second[e]

    def block(of):
        return band.at[:, pl.ds(pl.multiple_of(of * 64, 64), 64), :]

    sibling = (r, c ^ 1)
    chips = (4, 5, 3, 7, 1, 2, 6)
    early_sends = [
        pltpu.make_async_remote_copy(
            src_ref=early, dst_ref=block(c), send_sem=early_send.at[i], recv_sem=early_recv.at[i],
            device_id=sibling if i == 0 else (r, c ^ (2 * i)), device_id_type=MESH,
        )
        for i in chips + (0,)
    ]
    pl.semaphore_wait(
        barrier, 3 * has_north.astype(jnp.int32) + 3 * has_south.astype(jnp.int32) + cols - 1
    )

    for there, group in ((has_north, sends_north), (has_south, sends_south)):
        @pl.when(there)
        def _():
            for copy in group:
                copy.start()
    for copy in sends:
        copy.start()

    for core, order in ((0, (4, 5, 3, 7, 1, 2, 6, 0)), (1, (5, 3, 4, 7, 2, 1, 6, 0))):
        @pl.when(lax.rem(c, 2) == core)
        def _():
            for i in order:
                early_sends[chips.index(i) if i else 7].start()
    for copy in factor_copies:
        copy.start()

    wide_rows, wide_cols = 136, 256
    at_row = lax.broadcasted_iota(jnp.int32, (wide_rows, wide_cols), 0)
    at_col = lax.broadcasted_iota(jnp.int32, (wide_rows, wide_cols), 1)
    low_row = jnp.where(r == rows - 1, 128, 132)
    high_row = jnp.where(r == 0, 136, 132)
    low_col = jnp.where(c == cols - 1, 128, 192)
    high_col = jnp.where(c == 0, 256, 192)
    valid = ((at_row < low_row) | (at_row >= high_row)) & ((at_col < low_col) | (at_col >= high_col))
    upper_half = lax.broadcasted_iota(jnp.int32, (8, 128), 0) < 4
    left_half = lax.broadcasted_iota(jnp.int32, (8, 128), 1) < 64

    for copy in sends:
        copy.wait_recv()
    for i in range(3):
        from_side[i] = edge_cols[i].T
    for there, group in ((has_south, sends_north), (has_north, sends_south)):
        @pl.when(there)
        def _():
            for copy in group:
                copy.wait_recv()
    wide = []
    for i in range(3):
        under = jnp.where(upper_half, edge_rows[1, i], edge_rows[0, i])
        corner = jnp.where(
            left_half,
            jnp.where(upper_half, edge_rows[5, i], edge_rows[3, i]),
            jnp.where(upper_half, edge_rows[4, i], edge_rows[2, i]),
        )
        whole = jnp.concatenate(
            [jnp.concatenate([field[i], from_side[i]], axis=1), jnp.concatenate([under, corner], axis=1)], axis=0
        )
        wide.append(jnp.where(valid, whole, 0.0))
    current = passes(*wide, lambda v: jnp.where(valid, v, 0.0))
    middle[...] = current[:128, :128]

    own = pl.multiple_of(c * 64, 64)
    rows_of = [middle[pl.ds(i, 8, stride=TSIDE), :] * inside for i in range(TSIDE)]
    first, second = flat_tiles(rows_of)
    for e in range(8):
        band[0, pl.ds(own + e, 8, stride=8), :] = first[e]
        band[1, pl.ds(own + e, 8, stride=8), :] = second[e]

    at_lane = lax.broadcasted_iota(jnp.int32, (8, 128), 1)
    in_row = at_lane % TSIDE
    left_edge, right_edge = in_row < PASSES, in_row >= TSIDE - PASSES
    outer = left_edge | right_edge
    ends = [jnp.where(in_row < TSIDE // 2, half[0], half[7]) for half in (first, second)]
    patches[c, 0] = jnp.where(outer, ends[0], pltpu.roll(ends[1], 6, 1))
    patches[c, 1] = jnp.where(
        left_half, band[0, pl.ds(own, 8), :], band[1, pl.ds(pl.multiple_of(own + 56, 8), 8), :]
    )
    patch_sends = []
    for step in (10, 11, 6, 7, 14, 15, 8, 9, 4, 5, 12, 13, 2, 3, 1):
        copy = pltpu.make_async_remote_copy(
            src_ref=patches.at[c], dst_ref=patches.at[c],
            send_sem=patch_send.at[step], recv_sem=patch_recv.at[step],
            device_id=(r, c ^ step), device_id_type=MESH,
        )
        copy.start()
        patch_sends.append(copy)
    for i in range(TSIDE):
        results[0, pl.ds(i, 8, stride=TSIDE), :] = rows_of[i]

    passed = []
    for n, i in enumerate(chips):
        early_sends[n].wait_recv()
        copy = pltpu.make_async_remote_copy(
            src_ref=block(c ^ (2 * i)), dst_ref=block(c ^ (2 * i)),
            send_sem=pass_send.at[i], recv_sem=pass_recv.at[i],
            device_id=sibling, device_id_type=MESH,
        )
        copy.start()
        passed.append(copy)

    small_copies[1].wait()
    own_tiles = jnp.concatenate([band[h, pl.ds(own, 64), :] for h in range(2)], axis=1)
    own_term = lax.dot_general(
        own_tiles, self_kernel[...], (((1,), (1,)), ((), ())), precision=HIGHEST, preferred_element_type=F32
    )
    near[0], near[1] = own_term[:, :128], own_term[:, 128:]
    for copy in small_copies[2:]:
        copy.wait()
    for copy in factor_copies:
        copy.wait()

    at_rank = lax.broadcasted_iota(jnp.int32, (16, 256), 0)

    def cut(t, carry):
        for k in range(4):
            left[t, k] = jnp.where(at_rank < rank[k, t], left[t, k], 0.0)
        return carry

    lax.fori_loop(0, 64, cut, 0)
    for there, group in ((has_north, sends_north), (has_south, sends_south)):
        @pl.when(there)
        def _():
            for copy in group:
                copy.wait_send()
    for copy in sends + early_sends + patch_sends:
        copy.wait_send()
    for copy in patch_sends:
        copy.wait_recv()

    def patch(of):
        base = pl.multiple_of(of * 64, 64)
        columns = patches[of, 0]
        for h, value in ((0, columns), (1, pltpu.roll(columns, 122, 1))):
            for start, mask in ((base, left_edge), (base + 7, right_edge)):
                at = pl.ds(start, 8, stride=8)
                band[h, at, :] = jnp.where(mask, value, band[h, at, :])
        for h, start, mask in (
            (0, base, at_lane < PASSES * TSIDE), (1, base + 56, at_lane >= 128 - PASSES * TSIDE)
        ):
            at = pl.ds(pl.multiple_of(start, 8), 8)
            band[h, at, :] = jnp.where(mask, patches[of, 1], band[h, at, :])

    for i, copy in zip(chips, passed):
        copy.wait_send()
        patch(c ^ (2 * i))
    early_sends[-1].wait_recv()
    patch(c ^ 1)
    for i, copy in zip(chips, passed):
        copy.wait_recv()
        patch(c ^ (2 * i) ^ 1)

    ones = jnp.ones((256, 128), jnp.bfloat16)
    group = 64

    def interact(g, carry):
        highs, lows = [], []
        for u in range(group):
            t = g * group + u
            for k in range(4):
                at = column[k, t] * 64 + tile[k, t]
                factor = right[t, k]
                high, low = split_bf16(
                    factor[:, :128] * band[0, pl.ds(at, 1), :] + factor[:, 128:] * band[1, pl.ds(at, 1), :]
                )
                highs.append(high)
                lows.append(low)
        parts = jnp.concatenate([jnp.concatenate(highs, axis=0), jnp.concatenate(lows, axis=0)], axis=1)
        coefficients = jnp.dot(parts, ones, preferred_element_type=F32)
        sums = [[], []]
        for u in range(group):
            t = g * group + u
            factor = left[t].reshape(64, 256)
            scale = coefficients[u * 64:(u + 1) * 64]
            for h in range(2):
                sums[h].append(jnp.sum(factor[:, h * 128:(h + 1) * 128] * scale, axis=0, keepdims=True))
        at = pl.ds(pl.multiple_of(g * group, group), group)
        for h in range(2):
            near[h, at, :] = near[h, at, :] + jnp.concatenate(sums[h], axis=0)
        return carry

    lax.fori_loop(0, 64 // group, interact, 0)

    laid = []
    for h in range(2):
        laid += swap_blocks([near[h, pl.ds(e, 8, stride=8), :] for e in range(8)])
    for i in range(TSIDE):
        results[1, pl.ds(i, 8, stride=TSIDE), :] = laid[i]


def local(
    opening_old, pressure_old, injection, front_flags, self_kernel,
    source_column, source_tile, source_rank, left_factor, right_factor,
):
    rows, cols = lax.axis_size("row"), lax.axis_size("col")
    anywhere = pl.BlockSpec(memory_space=pl.ANY)
    out = jax.ShapeDtypeStruct((2, 128, 128), F32)
    lists = [a[0].T for a in (source_column, source_tile, source_rank)]
    operands = (opening_old, pressure_old, injection, front_flags, self_kernel, *lists, left_factor[0], right_factor[0])
    dma = pltpu.SemaphoreType.DMA
    both = pl.pallas_call(
        functools.partial(kernel, rows, cols),
        out_shape=out,
        in_specs=[anywhere] * 10,
        out_specs=pl.BlockSpec(memory_space=pltpu.VMEM),
        scratch_shapes=[
            pltpu.VMEM((3, 128, 128), F32),
            pltpu.VMEM((3, 128, 128), F32),
            pltpu.VMEM((3, 128, 128), F32),
            pltpu.VMEM((6, 3, 8, 128), F32),
            pltpu.VMEM((3, 128, 128), F32),
            pltpu.VMEM((128, 128), F32),
            pltpu.VMEM((2, 64, 128), F32),
            pltpu.VMEM((2, 64 * cols, 128), F32),
            pltpu.VMEM((cols, 2, 8, 128), F32),
            pltpu.VMEM((64, 4, 16, 256), F32),
            pltpu.VMEM((64, 4, 16, 256), F32),
            pltpu.VMEM((256, 256), F32),
            pltpu.VMEM((1, 64), jnp.int32),
            pltpu.VMEM((2, 64, 128), F32),
            pltpu.SMEM((4, 64), jnp.int32),
            pltpu.SMEM((4, 64), jnp.int32),
            pltpu.SMEM((4, 64), jnp.int32),
            dma((3,)),
            dma((5,)),
            dma((2,)),
            dma((8,)),
            dma((8,)),
            dma((8,)),
            dma((8,)),
            dma((8,)),
            dma((8,)),
            dma((16,)),
            dma((16,)),
        ],
        compiler_params=pltpu.CompilerParams(
            collective_id=0, has_side_effects=True, vmem_limit_bytes=40 * 1024 * 1024
        ),
        name="fracture",
    )(*[pltpu.with_memory_space_constraint(a, pltpu.HBM) for a in operands])
    return both[0], both[1]


def solution(mesh):
    fields, lists, factors = P("row", "col"), P("row", "col", None), P("row", "col", None, None, None)
    return jax.shard_map(
        local,
        mesh=mesh,
        in_specs=(fields, fields, fields, fields, P(), lists, lists, lists, factors, factors),
        out_specs=(fields, fields),
        check_vma=False,
    )
```
